32 devices in a mesh: grp: 4 (over x, core), usr: 8 (over z, y).
Axes of the slice: x: 2, y: 2, z: 4, core: 2. Of those that a mesh axis runs over, the one named last changes fastest.
Arguments:
- candidates: bfloat16 [8192, 1024], P(('grp', 'usr')), may hold values from -6 to 6
- hist_kv: bfloat16 [32, 384, 2048], P(('grp', 'usr')), may hold values from -6 to 6
- hist_len: int32 [32], P(('grp', 'usr')), may hold values from 1 to 384, as said below
- block_mask: int32 [32, 3], P(('grp', 'usr')), may hold values 0 or 1
- tile_user: int32 [128, 1], P(('grp', 'usr')), may hold values from 0 to 7; in each aligned block of 4 rows (0 to 3, 4 to 7, ...) no two rows name the same one
- tile_count: int32 [128], P(('grp', 'usr')), may hold values from 1 to 64, as said below
- weight_in: bfloat16 [1024, 4096], P(None, ('grp', 'usr')), may hold values from -0.1875 to 0.1875
- weight_out: bfloat16 [1024, 1024], P(('grp', 'usr')), may hold values from -0.1875 to 0.1875
Outputs:
- scored: bfloat16 [8192, 1024], P(('grp', 'usr'))
The draws below stay inside these ranges and needn't reach their ends.
Inputs may be any that keep to these rules, and one draw needn't show every extreme that they name: `hist_len`: some user's history has exactly 384 items. `tile_count`: the first tile of every device is full. A tile's live candidates take its first slots. `tile_user`: the tiles of one device belong to distinct users of its group.
All inputs are finite; a program needn't handle non-finite values. No bound on the sum of `block_mask` on one device may be relied on, other than what follows from the above.
Results may differ from the reference program's by a relative error of at most 0.0057.
Values may be sent and summed in bfloat16 or wider, within the bound.
A program may use at most 128 MiB of HBM per device.

```python
import math
import jax
import jax.numpy as jnp
import numpy as np
from jax import lax

D = 1024
HEADS = 8
HIST = 384
BLK = 128
NBLK = 3
TILE = 64
TILES_DEV = 4
USERS = 32
TILES = 128
CANDS = 8192
N_USR = 8
DEVICES = 32


def draw_hist_len(key, part):
    key = jax.random.fold_in(key, 11)
    lengths = jax.random.randint(key, (USERS,), 1, HIST + 1, dtype=jnp.int32)
    return lengths.at[0].set(HIST)


def draw_tile_count(key, part):
    key = jax.random.fold_in(key, 23)
    counts = jax.random.randint(key, (TILES,), 1, TILE + 1, dtype=jnp.int32)
    first_tile = jnp.arange(TILES, dtype=jnp.int32) % TILES_DEV == 0
    return jnp.where(first_tile, TILE, counts).astype(jnp.int32)


def touch_ends(entries, own_key, least, high):
    shape = entries.shape
    place = [jax.random.randint(jax.random.fold_in(own_key, axis), (), 0, shape[axis]) for axis in range(len(shape))]
    entries = entries.at[tuple(place)].set(least)
    longest = shape.index(max(shape))
    place[longest] = (place[longest] + 1) % shape[longest]
    return entries.at[tuple(place)].set(high)


def levels(key, shape, shards, low, largest):
    loudness = 1.0
    for position, blocks in shards:
        draws = jax.random.uniform(jax.random.fold_in(jax.random.fold_in(key, 6), position), (blocks,), jnp.float32, low / len(shards), largest / len(shards))
        loudness = loudness * jnp.repeat(jnp.exp(draws), shape[position] // blocks).reshape((-1,) + (1,) * (len(shape) - 1 - position))
    return loudness


def deal_out(own_key, own, number, rows, amount, top, most, skew):
    sequence = jax.random.permutation(own_key, amount)
    crowded, ordinary = load_shares(amount, rows * top, most, skew, True), load_shares(amount, rows * top, most, skew, False)
    places = jnp.arange(amount)

    def named(sizes, offset_by):
        used = int((sizes > 0).sum())
        fixed = max(1, used // 4)
        shifted = fixed + (places - fixed + offset_by * (used - fixed)) % max(1, amount - fixed)
        return jnp.zeros((amount,), jnp.int32).at[sequence[jnp.where(places < fixed, places, shifted)]].set(jnp.asarray(sizes, jnp.int32))

    sizes = jnp.where(number % 4 == 0, named(crowded, number // 4), named(ordinary, number - number // 4 - 1))
    mixed = jax.random.permutation(jax.random.fold_in(own, 3), amount)
    source_of, receiver = mixed[0:amount // 2 * 2:2], mixed[1:amount // 2 * 2:2]
    slack = jnp.minimum(sizes[source_of] - 1, most - sizes[receiver]) // 2
    slack = jnp.where((source_of == sequence[0]) | (receiver == sequence[0]) | (sizes[receiver] == 0), 0, jnp.maximum(slack, 0))
    shifted = jax.random.randint(jax.random.fold_in(own, 4), (amount // 2,), 0, 1 << 20) % (slack + 1)
    sizes = sizes.at[source_of].add(-shifted).at[receiver].add(shifted)
    labels = jnp.searchsorted(jnp.cumsum(sizes), jnp.arange(rows * top), side="right").astype(jnp.int32)
    grid = labels.reshape(top, rows).T
    grid = grid[jax.random.permutation(jax.random.fold_in(own, 1), rows)]
    offset_by = jax.random.randint(jax.random.fold_in(own, 2), (rows, 1), 0, top)
    return jnp.take_along_axis(grid, (jnp.arange(top)[None, :] + offset_by) % top, axis=1)


def load_shares(amount, total, most, skew, full):
    weights = [(1 << 20) // math.isqrt(grade ** skew) + 1 for grade in range(1, amount + 1)]
    largest = most if full else min(most, max(-(-total // amount), total * weights[0] // sum(weights)))
    least = 1 if total - largest >= amount - 1 else 0
    holding, surplus = [largest] + [least] * (amount - 1), total - largest - least * (amount - 1)
    while surplus > 0:
        movable = [i for i in range(1, amount) if holding[i] < largest] or [i for i in range(1, amount) if holding[i] < most]
        whole, left = sum([weights[i] for i in movable]), surplus
        for i in movable:
            extra = min(most - holding[i], max(1, left * weights[i] // whole), surplus)
            holding[i] = holding[i] + extra
            surplus = surplus - extra
    return np.array(holding)


def normal_values(rng, shape, deviation, reach, split=(), kind=jnp.bfloat16):
    factor_of = levels(rng, shape, split, -0.22, 0.18) if split else 1.0
    entries = jax.random.normal(rng, shape, jnp.float32) * deviation * factor_of
    return jnp.minimum(jnp.maximum(entries, -reach), reach).astype(kind)


def setup_inputs(seed: int = 0) -> dict:
    key_of = jax.random.split(jax.random.key(seed), 9)
    candidates = normal_values(key_of[0], (CANDS, D), 1.0, 6.0, ((0, 32),))
    hist_kv = normal_values(key_of[1], (USERS, HIST, 2 * D), 1.0, 6.0, ((0, 32),))
    hist_len = draw_hist_len(jax.random.fold_in(key_of[8], 71), 0)
    block_mask = touch_ends((jax.random.randint(key_of[3], (USERS, NBLK), 0, 4) < 3).astype(jnp.int32), jax.random.fold_in(key_of[3], 1), 0, 1)
    tile_user_keys = jax.random.split(jax.random.fold_in(key_of[4], 1), TILES // TILES_DEV)
    tile_user_turns = jax.random.permutation(jax.random.fold_in(key_of[4], 3), TILES // TILES_DEV)
    tile_user = jax.vmap(lambda own, number: deal_out(jax.random.fold_in(key_of[4], 2), own, number, TILES_DEV, N_USR, 1, 1, 2))(tile_user_keys, tile_user_turns).reshape((TILES, 1))
    tile_count = draw_tile_count(jax.random.fold_in(key_of[8], 71), 0)
    weight_in = normal_values(key_of[6], (D, 4 * D), D ** -0.5, 0.1875, ((1, 32),))
    weight_out = normal_values(key_of[7], (D, D), D ** -0.5, 0.1875, ((0, 32),))
    return dict(candidates=candidates, hist_kv=hist_kv, hist_len=hist_len, block_mask=block_mask, tile_user=tile_user, tile_count=tile_count, weight_in=weight_in, weight_out=weight_out)


def norm_rows(values_in):
    centred = values_in - lax.optimization_barrier(jnp.mean(values_in, axis=-1, keepdims=True))
    variance = lax.optimization_barrier(jnp.mean(centred * centred, axis=-1, keepdims=True))
    return centred * lax.rsqrt(variance + 1e-05)

def attend_rows(query_rows, hist_keys, hist_values, live_items, score_scale):
    row_total = query_rows.shape[0]
    model_width = query_rows.shape[1]
    head_dim = model_width // HEADS
    query_heads = query_rows.astype(jnp.float32).reshape(row_total, HEADS, head_dim)
    key_heads = hist_keys.astype(jnp.float32).reshape(-1, HEADS, head_dim)
    value_heads = hist_values.astype(jnp.float32).reshape(-1, HEADS, head_dim)
    scores = jnp.einsum('nhd,lhd->hnl', query_heads, key_heads) * score_scale
    weights = (jax.nn.silu(scores) * live_items).astype(jnp.bfloat16)
    attended = jnp.einsum('hnl,lhd->nhd', weights.astype(jnp.float32), value_heads)
    return attended.reshape(row_total, model_width)

def own_term(queries, self_keys, self_values, score_scale):
    row_total = queries.shape[0]
    products = (queries.astype(jnp.float32) * self_keys.astype(jnp.float32)).reshape(row_total, HEADS, -1)
    strength = jax.nn.silu(lax.optimization_barrier(jnp.sum(products, axis=2)) * score_scale)
    value_heads = self_values.astype(jnp.float32).reshape(row_total, HEADS, -1)
    return (strength[:, :, None] * value_heads).reshape(row_total, -1)

def reference(candidates, hist_kv, hist_len, block_mask, tile_user, tile_count, weight_in, weight_out):
    score_scale = (D // HEADS) ** (-0.5)
    positions = jnp.arange(HIST, dtype=jnp.int32)
    device_ids = jnp.arange(DEVICES, dtype=jnp.int32)
    group_base = device_ids // N_USR * N_USR
    rows_dev = candidates.reshape(DEVICES, TILES_DEV * TILE, D)
    users_dev = tile_user.reshape(DEVICES, TILES_DEV).astype(jnp.int32) + group_base[:, None]
    counts_dev = tile_count.reshape(DEVICES, TILES_DEV)

    def one_device(packed):
        cand_rows, tile_users, tile_counts = packed
        normed = norm_rows(cand_rows.astype(jnp.float32)).astype(jnp.bfloat16)
        projected = jax.nn.silu(jnp.dot(normed, weight_in, preferred_element_type=jnp.float32)).astype(jnp.bfloat16)
        queries = projected[:, :D]
        self_keys = projected[:, D:2 * D]
        self_values = projected[:, 2 * D:3 * D]
        gate_units = projected[:, 3 * D:]
        own_part = own_term(queries, self_keys, self_values, score_scale)

        def one_tile(packed_tile):
            tile_queries, user_id = packed_tile
            user_cache = lax.dynamic_index_in_dim(hist_kv, user_id, 0, keepdims=False)
            length = lax.dynamic_index_in_dim(hist_len, user_id, 0, keepdims=False)
            user_blocks = lax.dynamic_index_in_dim(block_mask, user_id, 0, keepdims=False)
            live_items = ((positions < length) & (jnp.repeat(user_blocks, BLK) > 0)).astype(jnp.float32)
            return attend_rows(tile_queries, user_cache[:, :D], user_cache[:, D:], live_items, score_scale).astype(jnp.bfloat16)
        history = lax.map(one_tile, (queries.reshape(TILES_DEV, TILE, D), tile_users)).reshape(TILES_DEV * TILE, D)
        combined = history.astype(jnp.float32) + own_part
        gated_rows = (norm_rows(combined) * gate_units.astype(jnp.float32)).astype(jnp.bfloat16)
        mixed_rows = jnp.dot(gated_rows, weight_out, preferred_element_type=jnp.float32) + cand_rows.astype(jnp.float32)
        live_rows = (jnp.arange(TILE, dtype=jnp.int32)[None, :] < tile_counts[:, None]).reshape(-1)
        return jnp.where(live_rows[:, None], mixed_rows, 0.0).astype(jnp.bfloat16)
    scored = lax.map(one_device, (rows_dev, users_dev, counts_dev))
    return scored.reshape(TILES * TILE, D)
```

```python
import functools
import math

import jax
import jax.numpy as jnp
from jax import lax
from jax.experimental import pallas as pl
from jax.experimental.pallas import tpu as pltpu
from jax.sharding import PartitionSpec as P

HEADS = 8
BLK = 128
MESH = pl.DeviceIdType.MESH


def norm_rows(values_in):
    centred = values_in - jnp.mean(values_in, axis=-1, keepdims=True)
    variance = jnp.mean(centred * centred, axis=-1, keepdims=True)
    return centred * lax.rsqrt(variance + 1e-05)


def attend_rows(query_rows, hist_keys, hist_values, live_items, score_scale):
    row_total = query_rows.shape[0]
    model_width = query_rows.shape[1]
    head_dim = model_width // HEADS
    query_heads = query_rows.reshape(row_total, HEADS, head_dim)
    key_heads = hist_keys.reshape(-1, HEADS, head_dim)
    value_heads = hist_values.reshape(-1, HEADS, head_dim)
    scores = (
        jnp.einsum("nhd,lhd->hnl", query_heads, key_heads, preferred_element_type=jnp.float32)
        * score_scale
    )
    weights = (jax.nn.silu(scores) * live_items).astype(jnp.bfloat16)
    attended = jnp.einsum("hnl,lhd->nhd", weights, value_heads, preferred_element_type=jnp.float32)
    return attended.reshape(row_total, model_width)


def own_term(queries, self_keys, self_values, score_scale):
    row_total = queries.shape[0]
    products = (queries.astype(jnp.float32) * self_keys.astype(jnp.float32)).reshape(
        row_total, HEADS, -1
    )
    strength = jax.nn.silu(jnp.sum(products, axis=2) * score_scale)
    value_heads = self_values.astype(jnp.float32).reshape(row_total, HEADS, -1)
    return (strength[:, :, None] * value_heads).reshape(row_total, -1)


def holder_attend(incoming, hist_keys, hist_values, live_items, score_scale):
    slot_total, item_count, model_width = incoming.shape
    per_group = math.gcd(slot_total, max(1, 512 // item_count))
    group_total = slot_total // per_group

    def answer_rows(row_block):
        return attend_rows(row_block, hist_keys, hist_values, live_items, score_scale).astype(
            jnp.bfloat16
        )

    row_blocks = incoming.reshape(group_total, per_group * item_count, model_width)
    answered = lax.map(answer_rows, row_blocks)
    return answered.reshape(slot_total, item_count, model_width)


def shards(candidates, hist_kv, hist_len, block_mask, tile_user, tile_count, weight_in, weight_out):
    row_total, model_width = candidates.shape
    tiles_here = tile_user.shape[0]
    tile_rows = row_total // tiles_here
    score_scale = (model_width // HEADS) ** (-0.5)
    holders = lax.axis_size("usr")
    normed = norm_rows(candidates.astype(jnp.float32)).astype(jnp.bfloat16)
    projected = jax.nn.silu(
        jnp.dot(
            normed,
            lax.all_gather(weight_in, ("grp", "usr"), axis=1, tiled=True),
            preferred_element_type=jnp.float32,
        )
    ).astype(jnp.bfloat16)
    queries = projected[:, :model_width]
    self_keys = projected[:, model_width : 2 * model_width]
    self_values = projected[:, 2 * model_width : 3 * model_width]
    gate_units = projected[:, 3 * model_width :]
    own_part = own_term(queries, self_keys, self_values, score_scale)
    tile_dest = tile_user[:, 0]
    outgoing = jnp.zeros((holders, tile_rows, model_width), jnp.bfloat16)
    outgoing = outgoing.at[tile_dest].set(queries.reshape(tiles_here, tile_rows, model_width))
    hist_keys = hist_kv[0, :, :model_width]
    hist_values = hist_kv[0, :, model_width:]
    positions = jnp.arange(hist_kv.shape[1], dtype=jnp.int32)
    live_items = ((positions < hist_len[0]) & (jnp.repeat(block_mask[0], BLK) > 0)).astype(
        jnp.float32
    )
    incoming = lax.all_to_all(outgoing, "usr", split_axis=0, concat_axis=0, tiled=True)
    returned = lax.all_to_all(
        holder_attend(incoming, hist_keys, hist_values, live_items, score_scale),
        "usr",
        split_axis=0,
        concat_axis=0,
        tiled=True,
    )
    history = returned[tile_dest].reshape(row_total, model_width)
    combined = history.astype(jnp.float32) + own_part
    gated_rows = (norm_rows(combined) * gate_units.astype(jnp.float32)).astype(jnp.bfloat16)
    mixed_rows = jnp.dot(
        gated_rows,
        lax.all_gather(weight_out, ("grp", "usr"), axis=0, tiled=True),
        preferred_element_type=jnp.float32,
    )
    mixed_rows = mixed_rows + candidates.astype(jnp.float32)
    live_rows = (jnp.arange(tile_rows, dtype=jnp.int32)[None, :] < tile_count[:, None]).reshape(-1)
    return jnp.where(live_rows[:, None], mixed_rows, 0.0).astype(jnp.bfloat16)


def silu(v):
    return v / (1.0 + jnp.exp(-v))


def layer_kernel(
    n_usr,
    cand_ref,
    kv_ref,
    len_ref,
    mask_ref,
    user_ref,
    count_ref,
    win_ref,
    wout_ref,
    out_ref,
    normed,
    w_all,
    wo_all,
    proj,
    own,
    outgoing,
    incoming,
    answers,
    returned,
    gated,
    w_recv,
    o_recv,
    w_send,
    o_send,
    q_recv,
    q_send,
    a_recv,
    a_send,
):
    depth, width = win_ref.shape
    out_rows = wout_ref.shape[0]
    row_total, model_width = cand_ref.shape
    tiles = user_ref.shape[0]
    tile_rows = row_total // tiles
    items = kv_ref.shape[1]
    scale = width ** (-0.5)
    g, u = lax.axis_index("grp"), lax.axis_index("usr")
    n_z = n_usr // 2
    x, c = g // 2, g % 2
    z, y = u // 2, u % 2
    to_x = ((1 - x) * 2 + c, u)
    to_c = (x * 2 + (1 - c), u)
    to_y = (g, z * 2 + (1 - y))

    def slot_of(xx, cc, yy, zz):
        return (xx * 2 + cc) * n_usr + zz * 2 + yy

    def w_copy(slot, part, target, sem):
        half = depth // 2
        lo, size = (0, depth) if part is None else (part * half, half)
        view = w_all.at[slot, pl.ds(lo, size), :]
        return pltpu.make_async_remote_copy(
            src_ref=view,
            dst_ref=view,
            send_sem=w_send.at[sem],
            recv_sem=w_recv.at[slot, part or 0],
            device_id=target,
            device_id_type=MESH,
        )

    def o_copy(slot, part, target, sem):
        half = out_rows // 2
        lo, size = (0, out_rows) if part is None else (part * half, half)
        view = wo_all.at[slot, pl.ds(lo, size), :]
        return pltpu.make_async_remote_copy(
            src_ref=view,
            dst_ref=view,
            send_sem=o_send.at[sem],
            recv_sem=o_recv.at[slot, part or 0],
            device_id=target,
            device_id_type=MESH,
        )

    def sends_own():
        me = slot_of(x, c, y, z)
        listed = [(me, None, (g, ((z + k) % n_z) * 2 + y), k - 1) for k in range(1, n_z)]
        return listed + [(me, None, to_x, 3), (me, None, to_y, 4), (me, None, to_c, 5)]

    def sends_line(k):
        slot = slot_of(x, c, y, (z + k) % n_z)
        base = 6 + (k - 1) * 3
        return [(slot, None, to_x, base), (slot, None, to_y, base + 1), (slot, None, to_c, base + 2)]

    def sends_y(k):
        slot = slot_of(x, c, 1 - y, (z + k) % n_z)
        base = 15 + k * 2
        return [(slot, 0, to_x, base), (slot, None, to_c, base + 1)]

    def sends_x(k):
        slot = slot_of(1 - x, c, y, (z + k) % n_z)
        base = 23 + k * 2
        return [(slot, 1, to_y, base), (slot, None, to_c, base + 1)]

    def sends_corner(k, part):
        slot = slot_of(1 - x, c, 1 - y, (z + k) % n_z)
        return [(slot, part, to_c, 31 + k * 2 + part)]

    def start_all(copy, listed):
        for entry in listed:
            copy(*entry).start()

    def arrived(copy, slot, part):
        copy(slot, part, to_c, 0).wait_recv()

    def relay(slot, part, listed):
        arrived(w_copy, slot, part)
        start_all(w_copy, listed)
        arrived(o_copy, slot, part)
        start_all(o_copy, listed)

    def project(slot):
        block = silu(jnp.dot(normed[...], w_all[slot], preferred_element_type=jnp.float32))
        proj[slot] = block.astype(jnp.bfloat16).reshape(tiles, tile_rows, width)

    barrier = pltpu.get_barrier_semaphore()
    peers = [to_x, to_c] + [(g, (u + k) % n_usr) for k in range(1, n_usr)]
    for peer in peers:
        pl.semaphore_signal(barrier, inc=1, device_id=peer, device_id_type=MESH)
    mine = slot_of(x, c, y, z)
    w_all[mine] = win_ref[...]
    wo_all[mine] = wout_ref[...]
    pl.semaphore_wait(barrier, len(peers))

    start_all(w_copy, sends_own())
    start_all(o_copy, sends_own())
    normed[...] = norm_rows(cand_ref[...].astype(jnp.float32)).astype(jnp.bfloat16)
    project(mine)

    def line_step(k, carry):
        slot = slot_of(x, c, y, (z + k) % n_z)
        relay(slot, None, sends_line(k))
        project(slot)
        return carry

    lax.fori_loop(1, n_z, line_step, 0)

    def take(slot, parts):
        for part in parts:
            arrived(w_copy, slot, part)
            arrived(o_copy, slot, part)
        project(slot)

    def side_step(k, carry):
        zz = (z + k) % n_z
        slot_y, slot_x = slot_of(x, c, 1 - y, zz), slot_of(1 - x, c, y, zz)
        relay(slot_y, None, sends_y(k))
        relay(slot_x, None, sends_x(k))
        project(slot_y)
        project(slot_x)
        take(slot_of(x, 1 - c, y, zz), (None,))
        return carry

    lax.fori_loop(0, n_z, side_step, 0)

    def corner_step(k, carry):
        zz = (z + k) % n_z
        slot = slot_of(1 - x, c, 1 - y, zz)
        for part in range(2):
            relay(slot, part, sends_corner(k, part))
        project(slot)
        take(slot_of(x, 1 - c, 1 - y, zz), (None,))
        take(slot_of(1 - x, 1 - c, y, zz), (None,))
        return carry

    lax.fori_loop(0, n_z, corner_step, 0)

    def last_step(k, carry):
        take(slot_of(1 - x, 1 - c, 1 - y, (z + k) % n_z), (0, 1))
        return carry

    lax.fori_loop(0, n_z, last_step, 0)

    def query_copy(k):
        holder = (u + k) % n_usr
        return pltpu.make_async_remote_copy(
            src_ref=outgoing.at[holder],
            dst_ref=incoming.at[u],
            send_sem=q_send.at[k],
            recv_sem=q_recv.at[k],
            device_id=(g, holder),
            device_id_type=MESH,
        )

    def answer_copy(k):
        source = (u + n_usr - k) % n_usr
        return pltpu.make_async_remote_copy(
            src_ref=answers.at[source],
            dst_ref=returned.at[u],
            send_sem=a_send.at[k],
            recv_sem=a_recv.at[k],
            device_id=(g, source),
            device_id_type=MESH,
        )

    def tile_for(holder):
        chosen = 0
        for t in range(tiles):
            chosen = jnp.where(user_ref[t, 0] == holder, t, chosen)
        return chosen

    def dispatch_step(k, carry):
        holder = (u + k) % n_usr
        tile = tile_for(holder)
        for h in range(HEADS):
            outgoing[holder, h] = proj[h, tile]
        query_copy(k).start()
        return carry

    lax.fori_loop(1, n_usr, dispatch_step, 0)
    own_tile = tile_for(u)
    for h in range(HEADS):
        incoming[u, h] = proj[h, own_tile]

    positions = lax.broadcasted_iota(jnp.int32, (1, items), 1)
    kept = jnp.zeros((1, items), jnp.int32)
    for b in range(items // BLK):
        kept = jnp.where(positions // BLK == b, mask_ref[0, b], kept)
    live = jnp.where((positions < len_ref[0]) & (kept > 0), 1.0, 0.0)

    def attend(slot, dest):
        for h in range(HEADS):
            keys = kv_ref[0, :, h * width : (h + 1) * width]
            values = kv_ref[0, :, model_width + h * width : model_width + (h + 1) * width]
            scores = lax.dot_general(
                incoming[slot, h], keys, (((1,), (1,)), ((), ())), preferred_element_type=jnp.float32
            )
            weights = (silu(scores * scale) * live).astype(jnp.bfloat16)
            dest[slot, h] = jnp.dot(weights, values, preferred_element_type=jnp.float32).astype(
                jnp.bfloat16
            )

    attend(u, returned)

    def own_step(h, carry):
        queries = proj[h].astype(jnp.float32)
        keys = proj[HEADS + h].astype(jnp.float32)
        strength = silu(jnp.sum(queries * keys, axis=-1, keepdims=True) * scale)
        own[h] = strength * proj[2 * HEADS + h].astype(jnp.float32)
        return carry

    lax.fori_loop(0, HEADS, own_step, 0)

    def answer_step(k, carry):
        query_copy(k).wait_recv()
        attend((u + n_usr - k) % n_usr, answers)
        answer_copy(k).start()
        return carry

    lax.fori_loop(1, n_usr, answer_step, 0)

    def return_step(k, carry):
        answer_copy(k).wait_recv()
        return carry

    lax.fori_loop(1, n_usr, return_step, 0)

    def tile_step(t, carry):
        holder = user_ref[t, 0]
        combined = jnp.concatenate(
            [returned[holder, h].astype(jnp.float32) + own[h, t] for h in range(HEADS)], axis=-1
        )
        units = jnp.concatenate([proj[3 * HEADS + h, t] for h in range(HEADS)], axis=-1)
        gated[t] = (norm_rows(combined) * units.astype(jnp.float32)).astype(jnp.bfloat16)
        return carry

    lax.fori_loop(0, tiles, tile_step, 0)

    slots_here = lax.broadcasted_iota(jnp.int32, (tile_rows, 1), 0)
    for lo in range(0, model_width, 256):
        weights = wo_all[:, :, lo : lo + 256].reshape(model_width, 256)
        mixed = jnp.dot(
            gated[...].reshape(row_total, model_width), weights, preferred_element_type=jnp.float32
        )
        for t in range(tiles):
            rows = slice(t * tile_rows, (t + 1) * tile_rows)
            total = mixed[rows] + cand_ref[rows, lo : lo + 256].astype(jnp.float32)
            out_ref[rows, lo : lo + 256] = jnp.where(slots_here < count_ref[t], total, 0.0).astype(
                jnp.bfloat16
            )

    def sent_all(listed):
        for entry in listed:
            w_copy(*entry).wait_send()
            o_copy(*entry).wait_send()

    def sent_line(k, carry):
        sent_all(sends_line(k))
        return carry

    def sent_rest(k, carry):
        sent_all(sends_y(k) + sends_x(k) + sends_corner(k, 0) + sends_corner(k, 1))
        return carry

    def sent_exchange(k, carry):
        query_copy(k).wait_send()
        answer_copy(k).wait_send()
        return carry

    sent_all(sends_own())
    lax.fori_loop(1, n_z, sent_line, 0)
    lax.fori_loop(0, n_z, sent_rest, 0)
    lax.fori_loop(1, n_usr, sent_exchange, 0)


def fused_shards(
    candidates, hist_kv, hist_len, block_mask, tile_user, tile_count, weight_in, weight_out
):
    row_total, model_width = candidates.shape
    n_usr, n_grp = lax.axis_size("usr"), lax.axis_size("grp")
    devices = n_usr * n_grp
    depth, width = weight_in.shape
    out_rows = weight_out.shape[0]
    tiles = tile_user.shape[0]
    tile_rows = row_total // tiles
    sends = 6 + 3 * (n_usr // 2 - 1) + 6 * (n_usr // 2)
    exchange = pltpu.VMEM((n_usr, HEADS, tile_rows, width), jnp.bfloat16)
    dma = pltpu.SemaphoreType.DMA
    in_vmem = pl.BlockSpec(memory_space=pltpu.VMEM)
    in_smem = pl.BlockSpec(memory_space=pltpu.SMEM)
    flops = 2 * row_total * model_width * model_width * 5 + 8 * n_usr * tile_rows * hist_kv.shape[1] * model_width
    return pl.pallas_call(
        functools.partial(layer_kernel, n_usr),
        out_shape=jax.ShapeDtypeStruct((row_total, model_width), jnp.bfloat16),
        in_specs=[in_vmem, in_vmem, in_smem, in_smem, in_smem, in_smem, in_vmem, in_vmem],
        out_specs=in_vmem,
        scratch_shapes=[
            pltpu.VMEM((row_total, model_width), jnp.bfloat16),
            pltpu.VMEM((devices, depth, width), jnp.bfloat16),
            pltpu.VMEM((devices, out_rows, model_width), jnp.bfloat16),
            pltpu.VMEM((devices, tiles, tile_rows, width), jnp.bfloat16),
            pltpu.VMEM((HEADS, tiles, tile_rows, width), jnp.float32),
            exchange,
            exchange,
            exchange,
            exchange,
            pltpu.VMEM((tiles, tile_rows, model_width), jnp.bfloat16),
            dma((devices, 2)),
            dma((devices, 2)),
            dma((sends,)),
            dma((sends,)),
            dma((n_usr,)),
            dma((n_usr,)),
            dma((n_usr,)),
            dma((n_usr,)),
        ],
        compiler_params=pltpu.CompilerParams(
            collective_id=0, has_side_effects=True, vmem_limit_bytes=48 * 1024 * 1024
        ),
        cost_estimate=pl.CostEstimate(flops=flops, bytes_accessed=4 * 1024 * 1024, transcendentals=0),
    )(candidates, hist_kv, hist_len, block_mask, tile_user, tile_count, weight_in, weight_out)


def solution(mesh):
    in_specs = (
        P(("grp", "usr"), None),
        P(("grp", "usr"), None, None),
        P(("grp", "usr")),
        P(("grp", "usr"), None),
        P(("grp", "usr"), None),
        P(("grp", "usr")),
        P(None, ("grp", "usr")),
        P(("grp", "usr"), None),
    )
    out_specs = P(("grp", "usr"), None)
    fits = mesh.shape["grp"] == 4 and mesh.shape["usr"] == HEADS
    body = fused_shards if fits else shards
    return jax.shard_map(body, mesh=mesh, in_specs=in_specs, out_specs=out_specs, check_vma=False)
```

```python
import functools
import math

import jax
import jax.numpy as jnp
from jax import lax
from jax.experimental import pallas as pl
from jax.experimental.pallas import tpu as pltpu
from jax.sharding import PartitionSpec as P

HEADS = 8
BLK = 128
MESH = pl.DeviceIdType.MESH


def norm_rows(values_in):
    centred = values_in - jnp.mean(values_in, axis=-1, keepdims=True)
    variance = jnp.mean(centred * centred, axis=-1, keepdims=True)
    return centred * lax.rsqrt(variance + 1e-05)


def attend_rows(query_rows, hist_keys, hist_values, live_items, score_scale):
    row_total = query_rows.shape[0]
    model_width = query_rows.shape[1]
    head_dim = model_width // HEADS
    query_heads = query_rows.reshape(row_total, HEADS, head_dim)
    key_heads = hist_keys.reshape(-1, HEADS, head_dim)
    value_heads = hist_values.reshape(-1, HEADS, head_dim)
    scores = (
        jnp.einsum("nhd,lhd->hnl", query_heads, key_heads, preferred_element_type=jnp.float32)
        * score_scale
    )
    weights = (jax.nn.silu(scores) * live_items).astype(jnp.bfloat16)
    attended = jnp.einsum("hnl,lhd->nhd", weights, value_heads, preferred_element_type=jnp.float32)
    return attended.reshape(row_total, model_width)


def own_term(queries, self_keys, self_values, score_scale):
    row_total = queries.shape[0]
    products = (queries.astype(jnp.float32) * self_keys.astype(jnp.float32)).reshape(
        row_total, HEADS, -1
    )
    strength = jax.nn.silu(jnp.sum(products, axis=2) * score_scale)
    value_heads = self_values.astype(jnp.float32).reshape(row_total, HEADS, -1)
    return (strength[:, :, None] * value_heads).reshape(row_total, -1)


def holder_attend(incoming, hist_keys, hist_values, live_items, score_scale):
    slot_total, item_count, model_width = incoming.shape
    per_group = math.gcd(slot_total, max(1, 512 // item_count))
    group_total = slot_total // per_group

    def answer_rows(row_block):
        return attend_rows(row_block, hist_keys, hist_values, live_items, score_scale).astype(
            jnp.bfloat16
        )

    row_blocks = incoming.reshape(group_total, per_group * item_count, model_width)
    answered = lax.map(answer_rows, row_blocks)
    return answered.reshape(slot_total, item_count, model_width)


def shards(candidates, hist_kv, hist_len, block_mask, tile_user, tile_count, weight_in, weight_out):
    row_total, model_width = candidates.shape
    tiles_here = tile_user.shape[0]
    tile_rows = row_total // tiles_here
    score_scale = (model_width // HEADS) ** (-0.5)
    holders = lax.axis_size("usr")
    normed = norm_rows(candidates.astype(jnp.float32)).astype(jnp.bfloat16)
    projected = jax.nn.silu(
        jnp.dot(
            normed,
            lax.all_gather(weight_in, ("grp", "usr"), axis=1, tiled=True),
            preferred_element_type=jnp.float32,
        )
    ).astype(jnp.bfloat16)
    queries = projected[:, :model_width]
    self_keys = projected[:, model_width : 2 * model_width]
    self_values = projected[:, 2 * model_width : 3 * model_width]
    gate_units = projected[:, 3 * model_width :]
    own_part = own_term(queries, self_keys, self_values, score_scale)
    tile_dest = tile_user[:, 0]
    outgoing = jnp.zeros((holders, tile_rows, model_width), jnp.bfloat16)
    outgoing = outgoing.at[tile_dest].set(queries.reshape(tiles_here, tile_rows, model_width))
    hist_keys = hist_kv[0, :, :model_width]
    hist_values = hist_kv[0, :, model_width:]
    positions = jnp.arange(hist_kv.shape[1], dtype=jnp.int32)
    live_items = ((positions < hist_len[0]) & (jnp.repeat(block_mask[0], BLK) > 0)).astype(
        jnp.float32
    )
    incoming = lax.all_to_all(outgoing, "usr", split_axis=0, concat_axis=0, tiled=True)
    returned = lax.all_to_all(
        holder_attend(incoming, hist_keys, hist_values, live_items, score_scale),
        "usr",
        split_axis=0,
        concat_axis=0,
        tiled=True,
    )
    history = returned[tile_dest].reshape(row_total, model_width)
    combined = history.astype(jnp.float32) + own_part
    gated_rows = (norm_rows(combined) * gate_units.astype(jnp.float32)).astype(jnp.bfloat16)
    mixed_rows = jnp.dot(
        gated_rows,
        lax.all_gather(weight_out, ("grp", "usr"), axis=0, tiled=True),
        preferred_element_type=jnp.float32,
    )
    mixed_rows = mixed_rows + candidates.astype(jnp.float32)
    live_rows = (jnp.arange(tile_rows, dtype=jnp.int32)[None, :] < tile_count[:, None]).reshape(-1)
    return jnp.where(live_rows[:, None], mixed_rows, 0.0).astype(jnp.bfloat16)


def silu(v):
    return v / (1.0 + jnp.exp(-v))


def layer_kernel(
    n_usr,
    cand_ref,
    kv_ref,
    len_ref,
    mask_ref,
    user_ref,
    count_ref,
    win_ref,
    wout_ref,
    out_ref,
    normed,
    w_all,
    wo_all,
    proj,
    own,
    outgoing,
    incoming,
    answers,
    returned,
    gated,
    w_recv,
    o_recv,
    w_send,
    o_send,
    q_recv,
    q_send,
    a_recv,
    a_send,
):
    depth, width = win_ref.shape
    out_rows = wout_ref.shape[0]
    row_total, model_width = cand_ref.shape
    tiles = user_ref.shape[0]
    tile_rows = row_total // tiles
    items = kv_ref.shape[1]
    scale = width ** (-0.5)
    g, u = lax.axis_index("grp"), lax.axis_index("usr")
    n_z = n_usr // 2
    x, c = g // 2, g % 2
    z, y = u // 2, u % 2
    to_x = ((1 - x) * 2 + c, u)
    to_c = (x * 2 + (1 - c), u)
    to_y = (g, z * 2 + (1 - y))

    def slot_of(xx, cc, yy, zz):
        return (xx * 2 + cc) * n_usr + zz * 2 + yy

    def w_copy(slot, part, target, sem):
        half = depth // 2
        lo, size = (0, depth) if part is None else (part * half, half)
        view = w_all.at[slot, pl.ds(lo, size), :]
        return pltpu.make_async_remote_copy(
            src_ref=view,
            dst_ref=view,
            send_sem=w_send.at[sem],
            recv_sem=w_recv.at[slot, part or 0],
            device_id=target,
            device_id_type=MESH,
        )

    def o_copy(slot, part, target, sem):
        half = out_rows // 2
        lo, size = (0, out_rows) if part is None else (part * half, half)
        view = wo_all.at[slot, pl.ds(lo, size), :]
        return pltpu.make_async_remote_copy(
            src_ref=view,
            dst_ref=view,
            send_sem=o_send.at[sem],
            recv_sem=o_recv.at[slot, part or 0],
            device_id=target,
            device_id_type=MESH,
        )

    is_query, x_is_query = (x == 0) & (c == 0), (x == 1) & (c == 0)
    sib_is_query, diagonal_is_query = (x == 0) & (c == 1), (x == 1) & (c == 1)

    def along_z(slot, zz, base):
        up, down = (zz <= z) & (z + 1 < n_z), (zz >= z) & (z > 0)
        return [
            (up, slot, None, (g, (z + 1) * 2 + y), base),
            (down, slot, None, (g, (z - 1) * 2 + y), base + 1),
        ]

    def sends_own():
        me = slot_of(x, c, y, z)
        return along_z(me, z, 0) + [(None, me, None, to_y, 2), (None, me, None, to_c, 3)]

    def sends_across():
        return [(None, slot_of(x, c, y, z), None, to_x, 4)]

    def sends_line(zz):
        slot = slot_of(x, c, y, zz)
        base = 5 + zz * 5
        return along_z(slot, zz, base) + [
            (None, slot, None, to_x, base + 2),
            (None, slot, None, to_y, base + 3),
            (None, slot, None, to_c, base + 4),
        ]

    def sends_y(k):
        slot = slot_of(x, c, 1 - y, (z + k) % n_z)
        base = 5 + n_z * 5 + k * 2
        return [(None, slot, 0, to_x, base), (None, slot, None, to_c, base + 1)]

    def sends_x(k):
        slot = slot_of(1 - x, c, y, (z + k) % n_z)
        base = 5 + n_z * 7 + k * 2
        return [(None, slot, 1, to_y, base), (None, slot, None, to_c, base + 1)]

    def sends_corner(k, part):
        slot = slot_of(1 - x, c, 1 - y, (z + k) % n_z)
        return [(None, slot, part, to_c, 5 + n_z * 9 + k * 2 + part)]

    def sends_query(zz):
        slot = slot_of(0, 0, y, zz)
        base = 5 + n_z * 11 + zz * 4
        return along_z(slot, zz, base) + [(None, slot, None, to_y, base + 2), (None, slot, None, to_c, base + 3)]

    def sends_query_y(k):
        slot = slot_of(0, 0, 1 - y, (z + k) % n_z)
        return [(None, slot, None, to_c, 5 + n_z * 15 + k)]

    def each(copy, listed, act):
        for needed, slot, part, target, sem in listed:
            if needed is None:
                act(copy(slot, part, target, sem))
            else:
                pl.when(needed)(lambda a=(slot, part, target, sem): act(copy(*a)))

    def start(descriptor):
        descriptor.start()

    def sent(descriptor):
        descriptor.wait_send()

    def arrived(copy, slot, part):
        copy(slot, part, to_c, 0).wait_recv()

    def project(slot):
        block = silu(jnp.dot(normed[...], w_all[slot], preferred_element_type=jnp.float32))
        proj[slot] = block.astype(jnp.bfloat16).reshape(tiles, tile_rows, width)

    def relay(slot, parts, listed, skip):
        @pl.when(jnp.logical_not(skip))
        def _():
            for part in parts:
                arrived(w_copy, slot, part)
                each(w_copy, [e for e in listed if len(parts) == 1 or e[2] == part], start)

        for part in parts:
            arrived(o_copy, slot, part)
            each(o_copy, [e for e in listed if len(parts) == 1 or e[2] == part], start)

        @pl.when(jnp.logical_not(skip))
        def _():
            project(slot)

    barrier = pltpu.get_barrier_semaphore()
    peers = [to_x, to_c] + [(g, (u + k) % n_usr) for k in range(1, n_usr)]
    for peer in peers:
        pl.semaphore_signal(barrier, inc=1, device_id=peer, device_id_type=MESH)
    mine = slot_of(x, c, y, z)
    w_all[mine] = win_ref[...]
    wo_all[mine] = wout_ref[...]
    pl.semaphore_wait(barrier, len(peers))

    each(w_copy, sends_across(), start)

    def query_relay(zz, known):
        slot = slot_of(0, 0, y, zz)

        @pl.when(jnp.logical_not(known))
        def _():
            arrived(w_copy, slot, None)

        @pl.when(c == 0)
        def _():
            each(w_copy, sends_query(zz), start)

    query_relay(z, is_query)
    normed[...] = norm_rows(cand_ref[...].astype(jnp.float32)).astype(jnp.bfloat16)
    project(slot_of(0, 0, y, z))

    def query_line(k, carry):
        for zz in (z - k, z + k):

            @pl.when((zz >= 0) & (zz < n_z))
            def _(zz=zz):
                query_relay(zz, False)
                project(slot_of(0, 0, y, zz))

        return carry

    lax.fori_loop(1, n_z, query_line, 0)

    def query_side(k, carry):
        slot = slot_of(0, 0, 1 - y, (z + k) % n_z)
        arrived(w_copy, slot, None)

        @pl.when(c == 0)
        def _():
            each(w_copy, sends_query_y(k), start)

        project(slot)
        return carry

    lax.fori_loop(0, n_z, query_side, 0)

    def query_copy(k):
        holder = (u + k) % n_usr
        return pltpu.make_async_remote_copy(
            src_ref=outgoing.at[holder],
            dst_ref=incoming.at[u],
            send_sem=q_send.at[k],
            recv_sem=q_recv.at[k],
            device_id=(g, holder),
            device_id_type=MESH,
        )

    def answer_copy(k):
        source = (u + n_usr - k) % n_usr
        return pltpu.make_async_remote_copy(
            src_ref=answers.at[source],
            dst_ref=returned.at[u],
            send_sem=a_send.at[k],
            recv_sem=a_recv.at[k],
            device_id=(g, source),
            device_id_type=MESH,
        )

    def tile_for(holder):
        chosen = 0
        for t in range(tiles):
            chosen = jnp.where(user_ref[t, 0] == holder, t, chosen)
        return chosen

    def dispatch_step(k, carry):
        holder = (u + k) % n_usr
        tile = tile_for(holder)
        for h in range(HEADS):
            outgoing[holder, h] = proj[h, tile]
        query_copy(k).start()
        return carry

    lax.fori_loop(1, n_usr, dispatch_step, 0)
    own_tile = tile_for(u)
    for h in range(HEADS):
        incoming[u, h] = proj[h, own_tile]

    positions = lax.broadcasted_iota(jnp.int32, (1, items), 1)
    kept = jnp.zeros((1, items), jnp.int32)
    for b in range(items // BLK):
        kept = jnp.where(positions // BLK == b, mask_ref[0, b], kept)
    live = jnp.where((positions < len_ref[0]) & (kept > 0), 1.0, 0.0)

    def attend(slot, dest):
        for h in range(HEADS):
            keys = kv_ref[0, :, h * width : (h + 1) * width]
            values = kv_ref[0, :, model_width + h * width : model_width + (h + 1) * width]
            scores = lax.dot_general(
                incoming[slot, h], keys, (((1,), (1,)), ((), ())), preferred_element_type=jnp.float32
            )
            weights = (silu(scores * scale) * live).astype(jnp.bfloat16)
            dest[slot, h] = jnp.dot(weights, values, preferred_element_type=jnp.float32).astype(
                jnp.bfloat16
            )

    @pl.when(jnp.logical_not(is_query))
    def _():
        each(w_copy, sends_own(), start)
        project(mine)

    each(o_copy, sends_own(), start)
    each(o_copy, sends_across(), start)

    attend(u, returned)

    def line_step(k, carry):
        for zz in (z - k, z + k):

            @pl.when((zz >= 0) & (zz < n_z))
            def _(zz=zz):
                relay(slot_of(x, c, y, zz), (None,), sends_line(zz), is_query)

        return carry

    lax.fori_loop(1, n_z, line_step, 0)

    def side_step(k, carry):
        zz = (z + k) % n_z
        relay(slot_of(x, c, 1 - y, zz), (None,), sends_y(k), is_query)
        relay(slot_of(1 - x, c, y, zz), (None,), sends_x(k), x_is_query)
        relay(slot_of(x, 1 - c, y, zz), (None,), [], sib_is_query)
        return carry

    lax.fori_loop(0, n_z, side_step, 0)

    def answer_step(k, carry):
        query_copy(k).wait_recv()
        attend((u + n_usr - k) % n_usr, answers)
        answer_copy(k).start()
        return carry

    lax.fori_loop(1, n_usr, answer_step, 0)

    def corner_step(k, carry):
        zz = (z + k) % n_z
        corner = sends_corner(k, 0) + sends_corner(k, 1)
        relay(slot_of(1 - x, c, 1 - y, zz), (0, 1), corner, x_is_query)
        relay(slot_of(x, 1 - c, 1 - y, zz), (None,), [], sib_is_query)
        relay(slot_of(1 - x, 1 - c, y, zz), (None,), [], diagonal_is_query)
        return carry

    lax.fori_loop(0, n_z, corner_step, 0)

    def last_step(k, carry):
        slot = slot_of(1 - x, 1 - c, 1 - y, (z + k) % n_z)
        relay(slot, (0, 1), [], diagonal_is_query)
        return carry

    lax.fori_loop(0, n_z, last_step, 0)

    def own_step(h, carry):
        queries = proj[h].astype(jnp.float32)
        keys = proj[HEADS + h].astype(jnp.float32)
        strength = silu(jnp.sum(queries * keys, axis=-1, keepdims=True) * scale)
        own[h] = strength * proj[2 * HEADS + h].astype(jnp.float32)
        return carry

    lax.fori_loop(0, HEADS, own_step, 0)

    def return_step(k, carry):
        answer_copy(k).wait_recv()
        return carry

    lax.fori_loop(1, n_usr, return_step, 0)

    def tile_step(t, carry):
        holder = user_ref[t, 0]
        combined = jnp.concatenate(
            [returned[holder, h].astype(jnp.float32) + own[h, t] for h in range(HEADS)], axis=-1
        )
        units = jnp.concatenate([proj[3 * HEADS + h, t] for h in range(HEADS)], axis=-1)
        gated[t] = (norm_rows(combined) * units.astype(jnp.float32)).astype(jnp.bfloat16)
        return carry

    lax.fori_loop(0, tiles, tile_step, 0)

    slots_here = lax.broadcasted_iota(jnp.int32, (tile_rows, 1), 0)
    for lo in range(0, model_width, 256):
        weights = wo_all[:, :, lo : lo + 256].reshape(model_width, 256)
        mixed = jnp.dot(
            gated[...].reshape(row_total, model_width), weights, preferred_element_type=jnp.float32
        )
        for t in range(tiles):
            rows = slice(t * tile_rows, (t + 1) * tile_rows)
            total = mixed[rows] + cand_ref[rows, lo : lo + 256].astype(jnp.float32)
            out_ref[rows, lo : lo + 256] = jnp.where(slots_here < count_ref[t], total, 0.0).astype(
                jnp.bfloat16
            )

    each(w_copy, sends_across(), sent)
    each(o_copy, sends_own() + sends_across(), sent)

    @pl.when(jnp.logical_not(is_query))
    def _():
        each(w_copy, sends_own(), sent)

    def sent_line(zz, carry):
        @pl.when(zz != z)
        def _():
            each(o_copy, sends_line(zz), sent)

        @pl.when((zz != z) & jnp.logical_not(is_query))
        def _():
            each(w_copy, sends_line(zz), sent)

        @pl.when(c == 0)
        def _():
            each(w_copy, sends_query(zz) + sends_query_y(zz), sent)

        return carry

    def sent_rest(k, carry):
        by_y, by_x = sends_y(k), sends_x(k) + sends_corner(k, 0) + sends_corner(k, 1)
        each(o_copy, by_y + by_x, sent)

        @pl.when(jnp.logical_not(is_query))
        def _():
            each(w_copy, by_y, sent)

        @pl.when(jnp.logical_not(x_is_query))
        def _():
            each(w_copy, by_x, sent)

        return carry

    def sent_exchange(k, carry):
        query_copy(k).wait_send()
        answer_copy(k).wait_send()
        return carry

    lax.fori_loop(0, n_z, sent_line, 0)
    lax.fori_loop(0, n_z, sent_rest, 0)
    lax.fori_loop(1, n_usr, sent_exchange, 0)


def fused_shards(
    candidates, hist_kv, hist_len, block_mask, tile_user, tile_count, weight_in, weight_out
):
    row_total, model_width = candidates.shape
    n_usr, n_grp = lax.axis_size("usr"), lax.axis_size("grp")
    devices = n_usr * n_grp
    depth, width = weight_in.shape
    out_rows = weight_out.shape[0]
    tiles = tile_user.shape[0]
    tile_rows = row_total // tiles
    sends = 5 + 16 * (n_usr // 2)
    exchange = pltpu.VMEM((n_usr, HEADS, tile_rows, width), jnp.bfloat16)
    dma = pltpu.SemaphoreType.DMA
    in_vmem = pl.BlockSpec(memory_space=pltpu.VMEM)
    in_smem = pl.BlockSpec(memory_space=pltpu.SMEM)
    flops = 2 * row_total * model_width * model_width * 5 + 8 * n_usr * tile_rows * hist_kv.shape[1] * model_width
    return pl.pallas_call(
        functools.partial(layer_kernel, n_usr),
        out_shape=jax.ShapeDtypeStruct((row_total, model_width), jnp.bfloat16),
        in_specs=[in_vmem, in_vmem, in_smem, in_smem, in_smem, in_smem, in_vmem, in_vmem],
        out_specs=in_vmem,
        scratch_shapes=[
            pltpu.VMEM((row_total, model_width), jnp.bfloat16),
            pltpu.VMEM((devices, depth, width), jnp.bfloat16),
            pltpu.VMEM((devices, out_rows, model_width), jnp.bfloat16),
            pltpu.VMEM((devices, tiles, tile_rows, width), jnp.bfloat16),
            pltpu.VMEM((HEADS, tiles, tile_rows, width), jnp.float32),
            exchange,
            exchange,
            exchange,
            exchange,
            pltpu.VMEM((tiles, tile_rows, model_width), jnp.bfloat16),
            dma((devices, 2)),
            dma((devices, 2)),
            dma((sends,)),
            dma((5 + 11 * (n_usr // 2),)),
            dma((n_usr,)),
            dma((n_usr,)),
            dma((n_usr,)),
            dma((n_usr,)),
        ],
        compiler_params=pltpu.CompilerParams(
            collective_id=0, has_side_effects=True, vmem_limit_bytes=48 * 1024 * 1024
        ),
        cost_estimate=pl.CostEstimate(flops=flops, bytes_accessed=4 * 1024 * 1024, transcendentals=0),
    )(candidates, hist_kv, hist_len, block_mask, tile_user, tile_count, weight_in, weight_out)


def solution(mesh):
    in_specs = (
        P(("grp", "usr"), None),
        P(("grp", "usr"), None, None),
        P(("grp", "usr")),
        P(("grp", "usr"), None),
        P(("grp", "usr"), None),
        P(("grp", "usr")),
        P(None, ("grp", "usr")),
        P(("grp", "usr"), None),
    )
    out_specs = P(("grp", "usr"), None)
    fits = mesh.shape["grp"] == 4 and mesh.shape["usr"] == HEADS
    body = fused_shards if fits else shards
    return jax.shard_map(body, mesh=mesh, in_specs=in_specs, out_specs=out_specs, check_vma=False)
```

```python
import functools
import math

import jax
import jax.numpy as jnp
from jax import lax
from jax.experimental import pallas as pl
from jax.experimental.pallas import tpu as pltpu
from jax.sharding import PartitionSpec as P

HEADS = 8
BLK = 128
MESH = pl.DeviceIdType.MESH


def norm_rows(values_in):
    centred = values_in - jnp.mean(values_in, axis=-1, keepdims=True)
    variance = jnp.mean(centred * centred, axis=-1, keepdims=True)
    return centred * lax.rsqrt(variance + 1e-05)


def attend_rows(query_rows, hist_keys, hist_values, live_items, score_scale):
    row_total = query_rows.shape[0]
    model_width = query_rows.shape[1]
    head_dim = model_width // HEADS
    query_heads = query_rows.reshape(row_total, HEADS, head_dim)
    key_heads = hist_keys.reshape(-1, HEADS, head_dim)
    value_heads = hist_values.reshape(-1, HEADS, head_dim)
    scores = (
        jnp.einsum("nhd,lhd->hnl", query_heads, key_heads, preferred_element_type=jnp.float32)
        * score_scale
    )
    weights = (jax.nn.silu(scores) * live_items).astype(jnp.bfloat16)
    attended = jnp.einsum("hnl,lhd->nhd", weights, value_heads, preferred_element_type=jnp.float32)
    return attended.reshape(row_total, model_width)


def own_term(queries, self_keys, self_values, score_scale):
    row_total = queries.shape[0]
    products = (queries.astype(jnp.float32) * self_keys.astype(jnp.float32)).reshape(
        row_total, HEADS, -1
    )
    strength = jax.nn.silu(jnp.sum(products, axis=2) * score_scale)
    value_heads = self_values.astype(jnp.float32).reshape(row_total, HEADS, -1)
    return (strength[:, :, None] * value_heads).reshape(row_total, -1)


def holder_attend(incoming, hist_keys, hist_values, live_items, score_scale):
    slot_total, item_count, model_width = incoming.shape
    per_group = math.gcd(slot_total, max(1, 512 // item_count))
    group_total = slot_total // per_group

    def answer_rows(row_block):
        return attend_rows(row_block, hist_keys, hist_values, live_items, score_scale).astype(
            jnp.bfloat16
        )

    row_blocks = incoming.reshape(group_total, per_group * item_count, model_width)
    answered = lax.map(answer_rows, row_blocks)
    return answered.reshape(slot_total, item_count, model_width)


def shards(candidates, hist_kv, hist_len, block_mask, tile_user, tile_count, weight_in, weight_out):
    row_total, model_width = candidates.shape
    tiles_here = tile_user.shape[0]
    tile_rows = row_total // tiles_here
    score_scale = (model_width // HEADS) ** (-0.5)
    holders = lax.axis_size("usr")
    normed = norm_rows(candidates.astype(jnp.float32)).astype(jnp.bfloat16)
    projected = jax.nn.silu(
        jnp.dot(
            normed,
            lax.all_gather(weight_in, ("grp", "usr"), axis=1, tiled=True),
            preferred_element_type=jnp.float32,
        )
    ).astype(jnp.bfloat16)
    queries = projected[:, :model_width]
    self_keys = projected[:, model_width : 2 * model_width]
    self_values = projected[:, 2 * model_width : 3 * model_width]
    gate_units = projected[:, 3 * model_width :]
    own_part = own_term(queries, self_keys, self_values, score_scale)
    tile_dest = tile_user[:, 0]
    outgoing = jnp.zeros((holders, tile_rows, model_width), jnp.bfloat16)
    outgoing = outgoing.at[tile_dest].set(queries.reshape(tiles_here, tile_rows, model_width))
    hist_keys = hist_kv[0, :, :model_width]
    hist_values = hist_kv[0, :, model_width:]
    positions = jnp.arange(hist_kv.shape[1], dtype=jnp.int32)
    live_items = ((positions < hist_len[0]) & (jnp.repeat(block_mask[0], BLK) > 0)).astype(
        jnp.float32
    )
    incoming = lax.all_to_all(outgoing, "usr", split_axis=0, concat_axis=0, tiled=True)
    returned = lax.all_to_all(
        holder_attend(incoming, hist_keys, hist_values, live_items, score_scale),
        "usr",
        split_axis=0,
        concat_axis=0,
        tiled=True,
    )
    history = returned[tile_dest].reshape(row_total, model_width)
    combined = history.astype(jnp.float32) + own_part
    gated_rows = (norm_rows(combined) * gate_units.astype(jnp.float32)).astype(jnp.bfloat16)
    mixed_rows = jnp.dot(
        gated_rows,
        lax.all_gather(weight_out, ("grp", "usr"), axis=0, tiled=True),
        preferred_element_type=jnp.float32,
    )
    mixed_rows = mixed_rows + candidates.astype(jnp.float32)
    live_rows = (jnp.arange(tile_rows, dtype=jnp.int32)[None, :] < tile_count[:, None]).reshape(-1)
    return jnp.where(live_rows[:, None], mixed_rows, 0.0).astype(jnp.bfloat16)


def silu(v):
    half = 0.5 * v
    return half + half * jnp.tanh(half)


def layer_kernel(
    n_usr,
    cand_hbm,
    kv_hbm,
    len_ref,
    mask_ref,
    user_ref,
    count_ref,
    win_hbm,
    wout_hbm,
    out_ref,
    cand_ref,
    kv_ref,
    key_heads,
    normed,
    w_all,
    wo_all,
    proj,
    own,
    outgoing,
    incoming,
    answers,
    returned,
    gated,
    w_recv,
    o_recv,
    w_send,
    o_send,
    q_recv,
    q_send,
    a_recv,
    a_send,
    load_sem,
):
    depth, width = win_hbm.shape
    out_rows = wout_hbm.shape[0]
    row_total, model_width = cand_ref.shape
    tiles = user_ref.shape[0]
    tile_rows = row_total // tiles
    items = kv_ref.shape[1]
    scale = width ** (-0.5)
    g, u = lax.axis_index("grp"), lax.axis_index("usr")
    n_z = n_usr // 2
    x, c = g // 2, g % 2
    z, y = u // 2, u % 2
    to_x = ((1 - x) * 2 + c, u)
    to_c = (x * 2 + (1 - c), u)
    to_y = (g, z * 2 + (1 - y))

    def slot_of(xx, cc, yy, zz):
        return (xx * 2 + cc) * n_usr + zz * 2 + yy

    def w_copy(slot, part, target, sem):
        half = depth // 2
        lo, size = (0, depth) if part is None else (part * half, half)
        view = w_all.at[slot, pl.ds(lo, size), :]
        return pltpu.make_async_remote_copy(
            src_ref=view,
            dst_ref=view,
            send_sem=w_send.at[sem],
            recv_sem=w_recv.at[slot, part or 0],
            device_id=target,
            device_id_type=MESH,
        )

    def o_copy(slot, part, target, sem):
        half = out_rows // 2
        lo, size = (0, out_rows) if part is None else (part * half, half)
        view = wo_all.at[slot, pl.ds(lo, size), :]
        return pltpu.make_async_remote_copy(
            src_ref=view,
            dst_ref=view,
            send_sem=o_send.at[sem],
            recv_sem=o_recv.at[slot, part or 0],
            device_id=target,
            device_id_type=MESH,
        )

    is_query, x_is_query = (x == 0) & (c == 0), (x == 1) & (c == 0)
    sib_is_query, diagonal_is_query = (x == 0) & (c == 1), (x == 1) & (c == 1)

    def along_z(slot, zz, base):
        up, down = (zz <= z) & (z + 1 < n_z), (zz >= z) & (z > 0)
        return [
            (up, slot, None, (g, (z + 1) * 2 + y), base),
            (down, slot, None, (g, (z - 1) * 2 + y), base + 1),
        ]

    def sends_own():
        me = slot_of(x, c, y, z)
        return along_z(me, z, 0) + [(None, me, None, to_y, 2), (None, me, None, to_c, 3)]

    def sends_across():
        return [(None, slot_of(x, c, y, z), None, to_x, 4)]

    def sends_query_across():
        return [(None, slot_of(0, 0, y, z), part, to_x, 5 + n_z * 11 + part) for part in range(2)]

    def sends_line(zz):
        slot = slot_of(x, c, y, zz)
        base = 5 + zz * 5
        return along_z(slot, zz, base) + [
            (None, slot, None, to_x, base + 2),
            (None, slot, None, to_y, base + 3),
            (None, slot, None, to_c, base + 4),
        ]

    def sends_y(k):
        slot = slot_of(x, c, 1 - y, (z + k) % n_z)
        base = 5 + n_z * 5 + k * 2
        return [(None, slot, 0, to_x, base), (None, slot, None, to_c, base + 1)]

    def sends_x(k):
        slot = slot_of(1 - x, c, y, (z + k) % n_z)
        base = 5 + n_z * 7 + k * 2
        return [(None, slot, 1, to_y, base), (None, slot, None, to_c, base + 1)]

    def sends_corner(k, part):
        slot = slot_of(1 - x, c, 1 - y, (z + k) % n_z)
        return [(None, slot, part, to_c, 5 + n_z * 9 + k * 2 + part)]

    def sends_query(zz, part):
        slot = slot_of(0, 0, y, zz)
        base = 7 + n_z * 11 + zz * 8 + part * 4
        up, down = (zz <= z) & (z + 1 < n_z), (zz >= z) & (z > 0)
        return [
            (up, slot, part, (g, (z + 1) * 2 + y), base),
            (down, slot, part, (g, (z - 1) * 2 + y), base + 1),
            (None, slot, part, to_y, base + 2),
            (None, slot, part, to_c, base + 3),
        ]

    def sends_query_y(k, part):
        slot = slot_of(0, 0, 1 - y, (z + k) % n_z)
        return [(None, slot, part, to_c, 7 + n_z * 19 + k * 2 + part)]

    def each(copy, listed, act):
        for needed, slot, part, target, sem in listed:
            if needed is None:
                act(copy(slot, part, target, sem))
            else:
                pl.when(needed)(lambda a=(slot, part, target, sem): act(copy(*a)))

    def start(descriptor):
        descriptor.start()

    def sent(descriptor):
        descriptor.wait_send()

    def arrived(copy, slot, part):
        copy(slot, part, to_c, 0).wait_recv()

    def project(slot):
        block = silu(jnp.dot(normed[...], w_all[slot], preferred_element_type=jnp.float32))
        proj[slot] = block.astype(jnp.bfloat16).reshape(tiles, tile_rows, width)

    def relay(slot, parts, listed, skip):
        @pl.when(jnp.logical_not(skip))
        def _():
            for part in parts:
                arrived(w_copy, slot, part)
                each(w_copy, [e for e in listed if len(parts) == 1 or e[2] == part], start)

        for part in parts:
            arrived(o_copy, slot, part)
            each(o_copy, [e for e in listed if len(parts) == 1 or e[2] == part], start)

        @pl.when(jnp.logical_not(skip))
        def _():
            project(slot)

    barrier = pltpu.get_barrier_semaphore()
    peers = [to_x, to_c] + [(g, (u + k) % n_usr) for k in range(1, n_usr)]
    for peer in peers:
        pl.semaphore_signal(barrier, inc=1, device_id=peer, device_id_type=MESH)
    mine = slot_of(x, c, y, z)
    loads = [
        pltpu.make_async_copy(cand_hbm, cand_ref, load_sem.at[0]),
        pltpu.make_async_copy(win_hbm, w_all.at[mine], load_sem.at[1]),
        pltpu.make_async_copy(wout_hbm, wo_all.at[mine], load_sem.at[2]),
        pltpu.make_async_copy(kv_hbm, kv_ref, load_sem.at[3]),
    ]
    for load in loads:
        load.start()
    loads[0].wait()
    normed[...] = norm_rows(cand_ref[...].astype(jnp.float32)).astype(jnp.bfloat16)
    loads[1].wait()
    pl.semaphore_wait(barrier, len(peers))

    @pl.when(is_query)
    def _():
        each(w_copy, sends_query_across(), start)

    @pl.when(jnp.logical_not(is_query))
    def _():
        each(w_copy, sends_across(), start)

    def query_relay(zz, known):
        slot = slot_of(0, 0, y, zz)

        for part in range(2):

            @pl.when(jnp.logical_not(known))
            def _(part=part):
                arrived(w_copy, slot, part)

            @pl.when(c == 0)
            def _(part=part):
                each(w_copy, sends_query(zz, part), start)

    query_relay(z, is_query)
    project(slot_of(0, 0, y, z))

    def query_line(k, carry):
        for zz in (z - k, z + k):

            @pl.when((zz >= 0) & (zz < n_z))
            def _(zz=zz):
                query_relay(zz, False)
                project(slot_of(0, 0, y, zz))

        return carry

    lax.fori_loop(1, n_z, query_line, 0)

    def query_side(k, carry):
        slot = slot_of(0, 0, 1 - y, (z + k) % n_z)
        for part in range(2):
            arrived(w_copy, slot, part)

            @pl.when(c == 0)
            def _(part=part):
                each(w_copy, sends_query_y(k, part), start)

        project(slot)
        return carry

    lax.fori_loop(0, n_z, query_side, 0)

    def query_copy(k):
        holder = ((z + k // 2) % n_z) * 2 + (y + k) % 2
        return pltpu.make_async_remote_copy(
            src_ref=outgoing.at[holder],
            dst_ref=incoming.at[u],
            send_sem=q_send.at[k],
            recv_sem=q_recv.at[k],
            device_id=(g, holder),
            device_id_type=MESH,
        )

    def source_of(k):
        return ((z + n_z - k // 2) % n_z) * 2 + (y + k) % 2

    def answer_copy(k):
        source = source_of(k)
        return pltpu.make_async_remote_copy(
            src_ref=answers.at[source],
            dst_ref=returned.at[u],
            send_sem=a_send.at[k],
            recv_sem=a_recv.at[k],
            device_id=(g, source),
            device_id_type=MESH,
        )

    def tile_for(holder):
        chosen = 0
        for t in range(tiles):
            chosen = jnp.where(user_ref[t, 0] == holder, t, chosen)
        return chosen

    def dispatch_step(k, carry):
        holder = ((z + k // 2) % n_z) * 2 + (y + k) % 2
        tile = tile_for(holder)
        for h in range(HEADS):
            outgoing[holder, h] = proj[h, tile]
        query_copy(k).start()
        return carry

    lax.fori_loop(1, n_usr, dispatch_step, 0)
    own_tile = tile_for(u)
    for h in range(HEADS):
        incoming[u, h] = proj[h, own_tile]

    positions = lax.broadcasted_iota(jnp.int32, (1, items), 1)
    kept = jnp.zeros((1, items), jnp.int32)
    for b in range(items // BLK):
        kept = jnp.where(positions // BLK == b, mask_ref[0, b], kept)
    live = jnp.where((positions < len_ref[0]) & (kept > 0), 1.0, 0.0)

    loads[3].wait()
    for h in range(HEADS):
        key_heads[h] = kv_ref[0, :, h * width : (h + 1) * width].T

    def attend(slot, dest):
        for h in range(HEADS):
            values = kv_ref[0, :, model_width + h * width : model_width + (h + 1) * width]
            scores = jnp.dot(incoming[slot, h], key_heads[h], preferred_element_type=jnp.float32)
            weights = (silu(scores * scale) * live).astype(jnp.bfloat16)
            dest[slot, h] = jnp.dot(weights, values, preferred_element_type=jnp.float32).astype(
                jnp.bfloat16
            )

    def answer(k):
        query_copy(k).wait_recv()
        attend(source_of(k), answers)
        answer_copy(k).start()

    @pl.when(jnp.logical_not(is_query))
    def _():
        each(w_copy, sends_own(), start)
        project(mine)

    loads[2].wait()
    each(o_copy, sends_own() + sends_across(), start)

    attend(u, returned)

    def line_step(k, carry):
        for zz in (z - k, z + k):

            @pl.when((zz >= 0) & (zz < n_z))
            def _(zz=zz):
                relay(slot_of(x, c, y, zz), (None,), sends_line(zz), is_query)

        answer(k)
        return carry

    lax.fori_loop(1, n_z, line_step, 0)

    def side_step(k, carry):
        zz = (z + k) % n_z
        relay(slot_of(x, c, 1 - y, zz), (None,), sends_y(k), is_query)
        relay(slot_of(1 - x, c, y, zz), (None,), sends_x(k), x_is_query)
        relay(slot_of(x, 1 - c, y, zz), (None,), [], sib_is_query)
        answer(n_z + k)
        return carry

    lax.fori_loop(0, n_z, side_step, 0)

    def corner_step(k, carry):
        zz = (z + k) % n_z
        corner = sends_corner(k, 0) + sends_corner(k, 1)
        relay(slot_of(1 - x, c, 1 - y, zz), (0, 1), corner, x_is_query)
        relay(slot_of(x, 1 - c, 1 - y, zz), (None,), [], sib_is_query)
        relay(slot_of(1 - x, 1 - c, y, zz), (None,), [], diagonal_is_query)
        return carry

    lax.fori_loop(0, n_z, corner_step, 0)

    def last_step(k, carry):
        slot = slot_of(1 - x, 1 - c, 1 - y, (z + k) % n_z)
        relay(slot, (0, 1), [], diagonal_is_query)
        return carry

    lax.fori_loop(0, n_z, last_step, 0)

    def own_step(h, carry):
        queries = proj[h].astype(jnp.float32)
        keys = proj[HEADS + h].astype(jnp.float32)
        strength = silu(jnp.sum(queries * keys, axis=-1, keepdims=True) * scale)
        own[h] = strength * proj[2 * HEADS + h].astype(jnp.float32)
        return carry

    lax.fori_loop(0, HEADS, own_step, 0)

    def return_step(k, carry):
        answer_copy(k).wait_recv()
        return carry

    lax.fori_loop(1, n_usr, return_step, 0)

    def tile_step(t, carry):
        holder = user_ref[t, 0]
        combined = jnp.concatenate(
            [returned[holder, h].astype(jnp.float32) + own[h, t] for h in range(HEADS)], axis=-1
        )
        units = jnp.concatenate([proj[3 * HEADS + h, t] for h in range(HEADS)], axis=-1)
        gated[t] = (norm_rows(combined) * units.astype(jnp.float32)).astype(jnp.bfloat16)
        return carry

    lax.fori_loop(0, tiles, tile_step, 0)

    slots_here = lax.broadcasted_iota(jnp.int32, (tile_rows, 1), 0)
    for lo in range(0, model_width, 256):
        weights = wo_all[:, :, lo : lo + 256].reshape(model_width, 256)
        mixed = jnp.dot(
            gated[...].reshape(row_total, model_width), weights, preferred_element_type=jnp.float32
        )
        for t in range(tiles):
            rows = slice(t * tile_rows, (t + 1) * tile_rows)
            total = mixed[rows] + cand_ref[rows, lo : lo + 256].astype(jnp.float32)
            out_ref[rows, lo : lo + 256] = jnp.where(slots_here < count_ref[t], total, 0.0).astype(
                jnp.bfloat16
            )

    @pl.when(is_query)
    def _():
        each(w_copy, sends_query_across(), sent)

    each(o_copy, sends_own() + sends_across(), sent)

    @pl.when(jnp.logical_not(is_query))
    def _():
        each(w_copy, sends_own() + sends_across(), sent)

    def sent_line(zz, carry):
        @pl.when(zz != z)
        def _():
            each(o_copy, sends_line(zz), sent)

        @pl.when((zz != z) & jnp.logical_not(is_query))
        def _():
            each(w_copy, sends_line(zz), sent)

        @pl.when(c == 0)
        def _():
            for part in range(2):
                each(w_copy, sends_query(zz, part) + sends_query_y(zz, part), sent)

        return carry

    def sent_rest(k, carry):
        by_y, by_x = sends_y(k), sends_x(k) + sends_corner(k, 0) + sends_corner(k, 1)
        each(o_copy, by_y + by_x, sent)

        @pl.when(jnp.logical_not(is_query))
        def _():
            each(w_copy, by_y, sent)

        @pl.when(jnp.logical_not(x_is_query))
        def _():
            each(w_copy, by_x, sent)

        return carry

    def sent_exchange(k, carry):
        query_copy(k).wait_send()
        answer_copy(k).wait_send()
        return carry

    lax.fori_loop(0, n_z, sent_line, 0)
    lax.fori_loop(0, n_z, sent_rest, 0)
    lax.fori_loop(1, n_usr, sent_exchange, 0)


def fused_shards(
    candidates, hist_kv, hist_len, block_mask, tile_user, tile_count, weight_in, weight_out
):
    row_total, model_width = candidates.shape
    n_usr, n_grp = lax.axis_size("usr"), lax.axis_size("grp")
    devices = n_usr * n_grp
    depth, width = weight_in.shape
    out_rows = weight_out.shape[0]
    tiles = tile_user.shape[0]
    tile_rows = row_total // tiles
    sends = 7 + 21 * (n_usr // 2)
    exchange = pltpu.VMEM((n_usr, HEADS, tile_rows, width), jnp.bfloat16)
    dma = pltpu.SemaphoreType.DMA
    in_any = pl.BlockSpec(memory_space=pl.ANY)
    in_vmem = pl.BlockSpec(memory_space=pltpu.VMEM)
    in_smem = pl.BlockSpec(memory_space=pltpu.SMEM)
    flops = 2 * row_total * model_width * model_width * 5 + 8 * n_usr * tile_rows * hist_kv.shape[1] * model_width
    return pl.pallas_call(
        functools.partial(layer_kernel, n_usr),
        out_shape=jax.ShapeDtypeStruct((row_total, model_width), jnp.bfloat16),
        in_specs=[in_any, in_any, in_smem, in_smem, in_smem, in_smem, in_any, in_any],
        out_specs=in_vmem,
        scratch_shapes=[
            pltpu.VMEM((row_total, model_width), jnp.bfloat16),
            pltpu.VMEM(hist_kv.shape, jnp.bfloat16),
            pltpu.VMEM((HEADS, width, hist_kv.shape[1]), jnp.bfloat16),
            pltpu.VMEM((row_total, model_width), jnp.bfloat16),
            pltpu.VMEM((devices, depth, width), jnp.bfloat16),
            pltpu.VMEM((devices, out_rows, model_width), jnp.bfloat16),
            pltpu.VMEM((devices, tiles, tile_rows, width), jnp.bfloat16),
            pltpu.VMEM((HEADS, tiles, tile_rows, width), jnp.float32),
            exchange,
            exchange,
            exchange,
            exchange,
            pltpu.VMEM((tiles, tile_rows, model_width), jnp.bfloat16),
            dma((devices, 2)),
            dma((devices, 2)),
            dma((sends,)),
            dma((5 + 11 * (n_usr // 2),)),
            dma((n_usr,)),
            dma((n_usr,)),
            dma((n_usr,)),
            dma((n_usr,)),
            dma((4,)),
        ],
        compiler_params=pltpu.CompilerParams(
            collective_id=0, has_side_effects=True, vmem_limit_bytes=60 * 1024 * 1024
        ),
        cost_estimate=pl.CostEstimate(flops=flops, bytes_accessed=4 * 1024 * 1024, transcendentals=0),
    )(candidates, hist_kv, hist_len, block_mask, tile_user, tile_count, weight_in, weight_out)


def solution(mesh):
    in_specs = (
        P(("grp", "usr"), None),
        P(("grp", "usr"), None, None),
        P(("grp", "usr")),
        P(("grp", "usr"), None),
        P(("grp", "usr"), None),
        P(("grp", "usr")),
        P(None, ("grp", "usr")),
        P(("grp", "usr"), None),
    )
    out_specs = P(("grp", "usr"), None)
    fits = mesh.shape["grp"] == 4 and mesh.shape["usr"] == HEADS
    body = fused_shards if fits else shards
    return jax.shard_map(body, mesh=mesh, in_specs=in_specs, out_specs=out_specs, check_vma=False)
```

```python
import functools
import math

import jax
import jax.numpy as jnp
from jax import lax
from jax.experimental import pallas as pl
from jax.experimental.pallas import tpu as pltpu
from jax.sharding import PartitionSpec as P

HEADS = 8
BLK = 128
MESH = pl.DeviceIdType.MESH


def norm_rows(values_in):
    centred = values_in - jnp.mean(values_in, axis=-1, keepdims=True)
    variance = jnp.mean(centred * centred, axis=-1, keepdims=True)
    return centred * lax.rsqrt(variance + 1e-05)


def attend_rows(query_rows, hist_keys, hist_values, live_items, score_scale):
    row_total = query_rows.shape[0]
    model_width = query_rows.shape[1]
    head_dim = model_width // HEADS
    query_heads = query_rows.reshape(row_total, HEADS, head_dim)
    key_heads = hist_keys.reshape(-1, HEADS, head_dim)
    value_heads = hist_values.reshape(-1, HEADS, head_dim)
    scores = (
        jnp.einsum("nhd,lhd->hnl", query_heads, key_heads, preferred_element_type=jnp.float32)
        * score_scale
    )
    weights = (jax.nn.silu(scores) * live_items).astype(jnp.bfloat16)
    attended = jnp.einsum("hnl,lhd->nhd", weights, value_heads, preferred_element_type=jnp.float32)
    return attended.reshape(row_total, model_width)


def own_term(queries, self_keys, self_values, score_scale):
    row_total = queries.shape[0]
    products = (queries.astype(jnp.float32) * self_keys.astype(jnp.float32)).reshape(
        row_total, HEADS, -1
    )
    strength = jax.nn.silu(jnp.sum(products, axis=2) * score_scale)
    value_heads = self_values.astype(jnp.float32).reshape(row_total, HEADS, -1)
    return (strength[:, :, None] * value_heads).reshape(row_total, -1)


def holder_attend(incoming, hist_keys, hist_values, live_items, score_scale):
    slot_total, item_count, model_width = incoming.shape
    per_group = math.gcd(slot_total, max(1, 512 // item_count))
    group_total = slot_total // per_group

    def answer_rows(row_block):
        return attend_rows(row_block, hist_keys, hist_values, live_items, score_scale).astype(
            jnp.bfloat16
        )

    row_blocks = incoming.reshape(group_total, per_group * item_count, model_width)
    answered = lax.map(answer_rows, row_blocks)
    return answered.reshape(slot_total, item_count, model_width)


def shards(candidates, hist_kv, hist_len, block_mask, tile_user, tile_count, weight_in, weight_out):
    row_total, model_width = candidates.shape
    tiles_here = tile_user.shape[0]
    tile_rows = row_total // tiles_here
    score_scale = (model_width // HEADS) ** (-0.5)
    holders = lax.axis_size("usr")
    normed = norm_rows(candidates.astype(jnp.float32)).astype(jnp.bfloat16)
    projected = jax.nn.silu(
        jnp.dot(
            normed,
            lax.all_gather(weight_in, ("grp", "usr"), axis=1, tiled=True),
            preferred_element_type=jnp.float32,
        )
    ).astype(jnp.bfloat16)
    queries = projected[:, :model_width]
    self_keys = projected[:, model_width : 2 * model_width]
    self_values = projected[:, 2 * model_width : 3 * model_width]
    gate_units = projected[:, 3 * model_width :]
    own_part = own_term(queries, self_keys, self_values, score_scale)
    tile_dest = tile_user[:, 0]
    outgoing = jnp.zeros((holders, tile_rows, model_width), jnp.bfloat16)
    outgoing = outgoing.at[tile_dest].set(queries.reshape(tiles_here, tile_rows, model_width))
    hist_keys = hist_kv[0, :, :model_width]
    hist_values = hist_kv[0, :, model_width:]
    positions = jnp.arange(hist_kv.shape[1], dtype=jnp.int32)
    live_items = ((positions < hist_len[0]) & (jnp.repeat(block_mask[0], BLK) > 0)).astype(
        jnp.float32
    )
    incoming = lax.all_to_all(outgoing, "usr", split_axis=0, concat_axis=0, tiled=True)
    returned = lax.all_to_all(
        holder_attend(incoming, hist_keys, hist_values, live_items, score_scale),
        "usr",
        split_axis=0,
        concat_axis=0,
        tiled=True,
    )
    history = returned[tile_dest].reshape(row_total, model_width)
    combined = history.astype(jnp.float32) + own_part
    gated_rows = (norm_rows(combined) * gate_units.astype(jnp.float32)).astype(jnp.bfloat16)
    mixed_rows = jnp.dot(
        gated_rows,
        lax.all_gather(weight_out, ("grp", "usr"), axis=0, tiled=True),
        preferred_element_type=jnp.float32,
    )
    mixed_rows = mixed_rows + candidates.astype(jnp.float32)
    live_rows = (jnp.arange(tile_rows, dtype=jnp.int32)[None, :] < tile_count[:, None]).reshape(-1)
    return jnp.where(live_rows[:, None], mixed_rows, 0.0).astype(jnp.bfloat16)


def silu(v):
    half = 0.5 * v
    return half + half * jnp.tanh(half)


def layer_kernel(
    n_usr,
    cand_hbm,
    kv_hbm,
    len_ref,
    mask_ref,
    user_ref,
    count_ref,
    win_hbm,
    wout_hbm,
    out_ref,
    cand_ref,
    kv_ref,
    key_heads,
    normed,
    w_all,
    wo_all,
    proj,
    own,
    outgoing,
    incoming,
    answers,
    returned,
    gated,
    w_recv,
    o_recv,
    w_send,
    o_send,
    q_recv,
    q_send,
    a_recv,
    a_send,
    load_sem,
):
    depth, width = win_hbm.shape
    out_rows = wout_hbm.shape[0]
    row_total, model_width = cand_ref.shape
    tiles = user_ref.shape[1]
    tile_rows = row_total // tiles
    items = kv_ref.shape[1]
    scale = width ** (-0.5)
    g, u = lax.axis_index("grp"), lax.axis_index("usr")
    n_z = n_usr // 2
    x, c = g // 2, g % 2
    z, y = u // 2, u % 2
    to_x = ((1 - x) * 2 + c, u)
    to_c = (x * 2 + (1 - c), u)
    to_y = (g, z * 2 + (1 - y))

    def slot_of(xx, cc, yy, zz):
        return (xx * 2 + cc) * n_usr + zz * 2 + yy

    def w_copy(slot, part, target, sem):
        half = depth // 2
        lo, size = (0, depth) if part is None else (part * half, half)
        view = w_all.at[slot, pl.ds(lo, size), :]
        return pltpu.make_async_remote_copy(
            src_ref=view,
            dst_ref=view,
            send_sem=w_send.at[sem],
            recv_sem=w_recv.at[slot, part or 0],
            device_id=target,
            device_id_type=MESH,
        )

    def o_copy(slot, part, target, sem):
        view = wo_all.at[slot]
        return pltpu.make_async_remote_copy(
            src_ref=view,
            dst_ref=view,
            send_sem=o_send.at[sem],
            recv_sem=o_recv.at[slot],
            device_id=target,
            device_id_type=MESH,
        )

    is_query, x_is_query = (x == 0) & (c == 0), (x == 1) & (c == 0)
    sib_is_query, diagonal_is_query = (x == 0) & (c == 1), (x == 1) & (c == 1)

    def along_z(slot, zz, base):
        up, down = (zz <= z) & (z + 1 < n_z), (zz >= z) & (z > 0)
        return [
            (up, slot, None, (g, (z + 1) * 2 + y), base),
            (down, slot, None, (g, (z - 1) * 2 + y), base + 1),
        ]

    def sends_own():
        me = slot_of(x, c, y, z)
        return along_z(me, z, 0) + [(None, me, None, to_y, 2), (None, me, None, to_c, 3)]

    def sends_across():
        return [(None, slot_of(x, c, y, z), None, to_x, 4)]

    def sends_line(zz):
        slot = slot_of(x, c, y, zz)
        base = 5 + zz * 5
        return along_z(slot, zz, base) + [
            (None, slot, None, to_x, base + 2),
            (None, slot, None, to_y, base + 3),
            (None, slot, None, to_c, base + 4),
        ]

    def sends_y(k):
        slot = slot_of(x, c, 1 - y, (z + k) % n_z)
        base = 5 + n_z * 5 + k * 2
        return [(None, slot, None, to_x, base), (None, slot, None, to_c, base + 1)]

    def sends_x(k):
        slot = slot_of(1 - x, c, y, (z + k) % n_z)
        return [(None, slot, None, to_c, 5 + n_z * 7 + k)]

    def sends_corner(k):
        slot = slot_of(1 - x, c, 1 - y, (z + k) % n_z)
        return [(None, slot, None, to_c, 5 + n_z * 8 + k)]

    def sends_query(zz, part):
        slot = slot_of(0, 0, y, zz)
        base = 5 + n_z * 9 + zz * 10 + part * 5
        up, down = (x == 0) & (zz <= z) & (z + 1 < n_z), (x == 0) & (zz >= z) & (z > 0)
        return [
            (up, slot, part, (g, (z + 1) * 2 + y), base),
            (down, slot, part, (g, (z - 1) * 2 + y), base + 1),
            (x == 0, slot, part, to_x, base + 2),
            (None, slot, part, to_y, base + 3),
            (None, slot, part, to_c, base + 4),
        ]

    def sends_query_y(k, part):
        slot = slot_of(0, 0, 1 - y, (z + k) % n_z)
        return [(None, slot, part, to_c, 5 + n_z * 19 + k * 2 + part)]

    def each(copy, listed, act):
        for needed, slot, part, target, sem in listed:
            if needed is None:
                act(copy(slot, part, target, sem))
            else:
                pl.when(needed)(lambda a=(slot, part, target, sem): act(copy(*a)))

    def start(descriptor):
        descriptor.start()

    def sent(descriptor):
        descriptor.wait_send()

    def arrived(copy, slot, part):
        copy(slot, part, to_c, 0).wait_recv()

    def project(slot):
        block = silu(jnp.dot(normed[...], w_all[slot], preferred_element_type=jnp.float32))
        proj[slot] = block.astype(jnp.bfloat16).reshape(tiles, tile_rows, width)

    def relay(slot, listed, skip):
        @pl.when(jnp.logical_not(skip))
        def _():
            arrived(w_copy, slot, None)
            each(w_copy, listed, start)

        arrived(o_copy, slot, None)
        each(o_copy, listed, start)

        @pl.when(jnp.logical_not(skip))
        def _():
            project(slot)

    barrier = pltpu.get_barrier_semaphore()
    peers = [to_x, to_c] + [(g, (u + k) % n_usr) for k in range(1, n_usr)]
    for peer in peers:
        pl.semaphore_signal(barrier, inc=1, device_id=peer, device_id_type=MESH)
    mine = slot_of(x, c, y, z)
    loads = [
        pltpu.make_async_copy(cand_hbm, cand_ref, load_sem.at[0]),
        pltpu.make_async_copy(win_hbm, w_all.at[mine], load_sem.at[1]),
        pltpu.make_async_copy(wout_hbm, wo_all.at[mine], load_sem.at[2]),
        pltpu.make_async_copy(kv_hbm, kv_ref, load_sem.at[3]),
    ]
    for load in loads:
        load.start()
    loads[0].wait()
    normed[...] = norm_rows(cand_ref[...].astype(jnp.float32)).astype(jnp.bfloat16)
    loads[1].wait()
    pl.semaphore_wait(barrier, len(peers))

    @pl.when(jnp.logical_not(is_query))
    def _():
        each(w_copy, sends_across(), start)

    def query_relay(zz, known):
        slot = slot_of(0, 0, y, zz)

        for part in range(2):

            @pl.when(jnp.logical_not(known))
            def _(part=part):
                arrived(w_copy, slot, part)

            @pl.when(c == 0)
            def _(part=part):
                each(w_copy, sends_query(zz, part), start)

    query_relay(z, is_query)
    project(slot_of(0, 0, y, z))

    def query_line(k, carry):
        for zz in (z - k, z + k):

            @pl.when((zz >= 0) & (zz < n_z))
            def _(zz=zz):
                query_relay(zz, False)
                project(slot_of(0, 0, y, zz))

        return carry

    lax.fori_loop(1, n_z, query_line, 0)

    def query_side(k, carry):
        slot = slot_of(0, 0, 1 - y, (z + k) % n_z)
        for part in range(2):
            arrived(w_copy, slot, part)

            @pl.when(c == 0)
            def _(part=part):
                each(w_copy, sends_query_y(k, part), start)

        project(slot)
        return carry

    lax.fori_loop(0, n_z, query_side, 0)

    def query_copy(k):
        holder = ((z + k // 2) % n_z) * 2 + (y + k) % 2
        return pltpu.make_async_remote_copy(
            src_ref=outgoing.at[holder],
            dst_ref=incoming.at[u],
            send_sem=q_send.at[k],
            recv_sem=q_recv.at[k],
            device_id=(g, holder),
            device_id_type=MESH,
        )

    def source_of(k):
        return ((z + n_z - k // 2) % n_z) * 2 + (y + k) % 2

    def answer_copy(k):
        source = source_of(k)
        return pltpu.make_async_remote_copy(
            src_ref=answers.at[source],
            dst_ref=returned.at[u],
            send_sem=a_send.at[k],
            recv_sem=a_recv.at[k],
            device_id=(g, source),
            device_id_type=MESH,
        )

    def tile_for(holder):
        chosen = 0
        for t in range(tiles):
            chosen = jnp.where(user_ref[0, t] == holder, t, chosen)
        return chosen

    def dispatch_step(k, carry):
        holder = ((z + k // 2) % n_z) * 2 + (y + k) % 2
        tile = tile_for(holder)
        for h in range(HEADS):
            outgoing[holder, h] = proj[h, tile]
        query_copy(k).start()
        return carry

    lax.fori_loop(1, n_usr, dispatch_step, 0)
    own_tile = tile_for(u)
    for h in range(HEADS):
        incoming[u, h] = proj[h, own_tile]

    positions = lax.broadcasted_iota(jnp.int32, (1, items), 1)
    kept = jnp.zeros((1, items), jnp.int32)
    for b in range(items // BLK):
        kept = jnp.where(positions // BLK == b, mask_ref[0, b], kept)
    live = jnp.where((positions < len_ref[0]) & (kept > 0), 1.0, 0.0)

    loads[3].wait()
    for h in range(HEADS):
        key_heads[h] = kv_ref[0, :, h * width : (h + 1) * width].T

    def attend(slot, dest):
        for h in range(HEADS):
            values = kv_ref[0, :, model_width + h * width : model_width + (h + 1) * width]
            scores = jnp.dot(incoming[slot, h], key_heads[h], preferred_element_type=jnp.float32)
            weights = (silu(scores * scale) * live).astype(jnp.bfloat16)
            dest[slot, h] = jnp.dot(weights, values, preferred_element_type=jnp.float32).astype(
                jnp.bfloat16
            )

    def answer(k):
        query_copy(k).wait_recv()
        attend(source_of(k), answers)
        answer_copy(k).start()

    @pl.when(jnp.logical_not(is_query))
    def _():
        each(w_copy, sends_own(), start)
        project(mine)

    loads[2].wait()
    each(o_copy, sends_own() + sends_across(), start)

    attend(u, returned)

    def line_step(k, carry):
        for zz in (z - k, z + k):

            @pl.when((zz >= 0) & (zz < n_z))
            def _(zz=zz):
                relay(slot_of(x, c, y, zz), sends_line(zz), is_query)

        answer(k)
        return carry

    lax.fori_loop(1, n_z, line_step, 0)

    def side_step(k, carry):
        zz = (z + k) % n_z
        relay(slot_of(x, c, 1 - y, zz), sends_y(k), is_query)
        relay(slot_of(1 - x, c, y, zz), sends_x(k), x_is_query)
        relay(slot_of(x, 1 - c, y, zz), [], sib_is_query)
        answer(n_z + k)
        return carry

    lax.fori_loop(0, n_z, side_step, 0)

    def corner_step(k, carry):
        zz = (z + k) % n_z
        relay(slot_of(1 - x, c, 1 - y, zz), sends_corner(k), x_is_query)
        relay(slot_of(x, 1 - c, 1 - y, zz), [], sib_is_query)
        relay(slot_of(1 - x, 1 - c, y, zz), [], diagonal_is_query)
        return carry

    lax.fori_loop(0, n_z, corner_step, 0)

    def last_step(k, carry):
        slot = slot_of(1 - x, 1 - c, 1 - y, (z + k) % n_z)
        relay(slot, [], diagonal_is_query)
        return carry

    lax.fori_loop(0, n_z, last_step, 0)

    def own_step(h, carry):
        queries = proj[h].astype(jnp.float32)
        keys = proj[HEADS + h].astype(jnp.float32)
        strength = silu(jnp.sum(queries * keys, axis=-1, keepdims=True) * scale)
        own[h] = strength * proj[2 * HEADS + h].astype(jnp.float32)
        return carry

    lax.fori_loop(0, HEADS, own_step, 0)

    def return_step(k, carry):
        answer_copy(k).wait_recv()
        return carry

    lax.fori_loop(1, n_usr, return_step, 0)

    def tile_step(t, carry):
        holder = user_ref[0, t]
        combined = jnp.concatenate(
            [returned[holder, h].astype(jnp.float32) + own[h, t] for h in range(HEADS)], axis=-1
        )
        units = jnp.concatenate([proj[3 * HEADS + h, t] for h in range(HEADS)], axis=-1)
        gated[t] = (norm_rows(combined) * units.astype(jnp.float32)).astype(jnp.bfloat16)
        return carry

    lax.fori_loop(0, tiles, tile_step, 0)

    slots_here = lax.broadcasted_iota(jnp.int32, (tile_rows, 1), 0)
    for lo in range(0, model_width, 256):
        weights = wo_all[:, :, lo : lo + 256].reshape(model_width, 256)
        mixed = jnp.dot(
            gated[...].reshape(row_total, model_width), weights, preferred_element_type=jnp.float32
        )
        for t in range(tiles):
            rows = slice(t * tile_rows, (t + 1) * tile_rows)
            total = mixed[rows] + cand_ref[rows, lo : lo + 256].astype(jnp.float32)
            out_ref[rows, lo : lo + 256] = jnp.where(slots_here < count_ref[t], total, 0.0).astype(
                jnp.bfloat16
            )

    each(o_copy, sends_own() + sends_across(), sent)

    @pl.when(jnp.logical_not(is_query))
    def _():
        each(w_copy, sends_own() + sends_across(), sent)

    def sent_line(zz, carry):
        @pl.when(zz != z)
        def _():
            each(o_copy, sends_line(zz), sent)

        @pl.when((zz != z) & jnp.logical_not(is_query))
        def _():
            each(w_copy, sends_line(zz), sent)

        @pl.when(c == 0)
        def _():
            for part in range(2):
                each(w_copy, sends_query(zz, part) + sends_query_y(zz, part), sent)

        return carry

    def sent_rest(k, carry):
        by_y, by_x = sends_y(k), sends_x(k) + sends_corner(k)
        each(o_copy, by_y + by_x, sent)

        @pl.when(jnp.logical_not(is_query))
        def _():
            each(w_copy, by_y, sent)

        @pl.when(jnp.logical_not(x_is_query))
        def _():
            each(w_copy, by_x, sent)

        return carry

    def sent_exchange(k, carry):
        query_copy(k).wait_send()
        answer_copy(k).wait_send()
        return carry

    lax.fori_loop(0, n_z, sent_line, 0)
    lax.fori_loop(0, n_z, sent_rest, 0)
    lax.fori_loop(1, n_usr, sent_exchange, 0)


def fused_shards(
    candidates, hist_kv, hist_len, block_mask, tile_user, tile_count, weight_in, weight_out
):
    row_total, model_width = candidates.shape
    n_usr, n_grp = lax.axis_size("usr"), lax.axis_size("grp")
    devices = n_usr * n_grp
    depth, width = weight_in.shape
    out_rows = weight_out.shape[0]
    tiles = tile_user.shape[0]
    tile_rows = row_total // tiles
    sends = 5 + 21 * (n_usr // 2)
    exchange = pltpu.VMEM((n_usr, HEADS, tile_rows, width), jnp.bfloat16)
    dma = pltpu.SemaphoreType.DMA
    in_any = pl.BlockSpec(memory_space=pl.ANY)
    in_vmem = pl.BlockSpec(memory_space=pltpu.VMEM)
    in_smem = pl.BlockSpec(memory_space=pltpu.SMEM)
    flops = 2 * row_total * model_width * model_width * 5 + 8 * n_usr * tile_rows * hist_kv.shape[1] * model_width
    return pl.pallas_call(
        functools.partial(layer_kernel, n_usr),
        out_shape=jax.ShapeDtypeStruct((row_total, model_width), jnp.bfloat16),
        in_specs=[in_any, in_any, in_smem, in_smem, in_smem, in_smem, in_any, in_any],
        out_specs=in_vmem,
        scratch_shapes=[
            pltpu.VMEM((row_total, model_width), jnp.bfloat16),
            pltpu.VMEM(hist_kv.shape, jnp.bfloat16),
            pltpu.VMEM((HEADS, width, hist_kv.shape[1]), jnp.bfloat16),
            pltpu.VMEM((row_total, model_width), jnp.bfloat16),
            pltpu.VMEM((devices, depth, width), jnp.bfloat16),
            pltpu.VMEM((devices, out_rows, model_width), jnp.bfloat16),
            pltpu.VMEM((devices, tiles, tile_rows, width), jnp.bfloat16),
            pltpu.VMEM((HEADS, tiles, tile_rows, width), jnp.float32),
            exchange,
            exchange,
            exchange,
            exchange,
            pltpu.VMEM((tiles, tile_rows, model_width), jnp.bfloat16),
            dma((devices, 2)),
            dma((devices,)),
            dma((sends,)),
            dma((5 + 9 * (n_usr // 2),)),
            dma((n_usr,)),
            dma((n_usr,)),
            dma((n_usr,)),
            dma((n_usr,)),
            dma((4,)),
        ],
        compiler_params=pltpu.CompilerParams(
            collective_id=0, has_side_effects=True, vmem_limit_bytes=60 * 1024 * 1024
        ),
        cost_estimate=pl.CostEstimate(flops=flops, bytes_accessed=4 * 1024 * 1024, transcendentals=0),
    )(candidates, hist_kv, hist_len, block_mask, tile_user.T, tile_count, weight_in, weight_out)


def solution(mesh):
    in_specs = (
        P(("grp", "usr"), None),
        P(("grp", "usr"), None, None),
        P(("grp", "usr")),
        P(("grp", "usr"), None),
        P(("grp", "usr"), None),
        P(("grp", "usr")),
        P(None, ("grp", "usr")),
        P(("grp", "usr"), None),
    )
    out_specs = P(("grp", "usr"), None)
    fits = mesh.shape["grp"] == 4 and mesh.shape["usr"] == HEADS
    body = fused_shards if fits else shards
    return jax.shard_map(body, mesh=mesh, in_specs=in_specs, out_specs=out_specs, check_vma=False)
```

```python
import functools
import math

import jax
import jax.numpy as jnp
from jax import lax
from jax.experimental import pallas as pl
from jax.experimental.pallas import tpu as pltpu
from jax.sharding import PartitionSpec as P

HEADS = 8
BLK = 128
MESH = pl.DeviceIdType.MESH


def norm_rows(values_in):
    centred = values_in - jnp.mean(values_in, axis=-1, keepdims=True)
    variance = jnp.mean(centred * centred, axis=-1, keepdims=True)
    return centred * lax.rsqrt(variance + 1e-05)


def attend_rows(query_rows, hist_keys, hist_values, live_items, score_scale):
    row_total = query_rows.shape[0]
    model_width = query_rows.shape[1]
    head_dim = model_width // HEADS
    query_heads = query_rows.reshape(row_total, HEADS, head_dim)
    key_heads = hist_keys.reshape(-1, HEADS, head_dim)
    value_heads = hist_values.reshape(-1, HEADS, head_dim)
    scores = (
        jnp.einsum("nhd,lhd->hnl", query_heads, key_heads, preferred_element_type=jnp.float32)
        * score_scale
    )
    weights = (jax.nn.silu(scores) * live_items).astype(jnp.bfloat16)
    attended = jnp.einsum("hnl,lhd->nhd", weights, value_heads, preferred_element_type=jnp.float32)
    return attended.reshape(row_total, model_width)


def own_term(queries, self_keys, self_values, score_scale):
    row_total = queries.shape[0]
    products = (queries.astype(jnp.float32) * self_keys.astype(jnp.float32)).reshape(
        row_total, HEADS, -1
    )
    strength = jax.nn.silu(jnp.sum(products, axis=2) * score_scale)
    value_heads = self_values.astype(jnp.float32).reshape(row_total, HEADS, -1)
    return (strength[:, :, None] * value_heads).reshape(row_total, -1)


def holder_attend(incoming, hist_keys, hist_values, live_items, score_scale):
    slot_total, item_count, model_width = incoming.shape
    per_group = math.gcd(slot_total, max(1, 512 // item_count))
    group_total = slot_total // per_group

    def answer_rows(row_block):
        return attend_rows(row_block, hist_keys, hist_values, live_items, score_scale).astype(
            jnp.bfloat16
        )

    row_blocks = incoming.reshape(group_total, per_group * item_count, model_width)
    answered = lax.map(answer_rows, row_blocks)
    return answered.reshape(slot_total, item_count, model_width)


def shards(candidates, hist_kv, hist_len, block_mask, tile_user, tile_count, weight_in, weight_out):
    row_total, model_width = candidates.shape
    tiles_here = tile_user.shape[0]
    tile_rows = row_total // tiles_here
    score_scale = (model_width // HEADS) ** (-0.5)
    holders = lax.axis_size("usr")
    normed = norm_rows(candidates.astype(jnp.float32)).astype(jnp.bfloat16)
    projected = jax.nn.silu(
        jnp.dot(
            normed,
            lax.all_gather(weight_in, ("grp", "usr"), axis=1, tiled=True),
            preferred_element_type=jnp.float32,
        )
    ).astype(jnp.bfloat16)
    queries = projected[:, :model_width]
    self_keys = projected[:, model_width : 2 * model_width]
    self_values = projected[:, 2 * model_width : 3 * model_width]
    gate_units = projected[:, 3 * model_width :]
    own_part = own_term(queries, self_keys, self_values, score_scale)
    tile_dest = tile_user[:, 0]
    outgoing = jnp.zeros((holders, tile_rows, model_width), jnp.bfloat16)
    outgoing = outgoing.at[tile_dest].set(queries.reshape(tiles_here, tile_rows, model_width))
    hist_keys = hist_kv[0, :, :model_width]
    hist_values = hist_kv[0, :, model_width:]
    positions = jnp.arange(hist_kv.shape[1], dtype=jnp.int32)
    live_items = ((positions < hist_len[0]) & (jnp.repeat(block_mask[0], BLK) > 0)).astype(
        jnp.float32
    )
    incoming = lax.all_to_all(outgoing, "usr", split_axis=0, concat_axis=0, tiled=True)
    returned = lax.all_to_all(
        holder_attend(incoming, hist_keys, hist_values, live_items, score_scale),
        "usr",
        split_axis=0,
        concat_axis=0,
        tiled=True,
    )
    history = returned[tile_dest].reshape(row_total, model_width)
    combined = history.astype(jnp.float32) + own_part
    gated_rows = (norm_rows(combined) * gate_units.astype(jnp.float32)).astype(jnp.bfloat16)
    mixed_rows = jnp.dot(
        gated_rows,
        lax.all_gather(weight_out, ("grp", "usr"), axis=0, tiled=True),
        preferred_element_type=jnp.float32,
    )
    mixed_rows = mixed_rows + candidates.astype(jnp.float32)
    live_rows = (jnp.arange(tile_rows, dtype=jnp.int32)[None, :] < tile_count[:, None]).reshape(-1)
    return jnp.where(live_rows[:, None], mixed_rows, 0.0).astype(jnp.bfloat16)


def silu(v):
    half = 0.5 * v
    return half + half * jnp.tanh(half)


def layer_kernel(
    n_usr,
    cand_hbm,
    kv_hbm,
    len_ref,
    mask_ref,
    user_ref,
    count_ref,
    win_hbm,
    wout_hbm,
    out_ref,
    cand_ref,
    kv_ref,
    key_heads,
    normed,
    w_all,
    wo_all,
    proj,
    own,
    outgoing,
    incoming,
    answers,
    returned,
    gated,
    w_recv,
    o_recv,
    w_send,
    o_send,
    q_recv,
    q_send,
    a_recv,
    a_send,
    load_sem,
):
    depth, width = win_hbm.shape
    out_rows = wout_hbm.shape[0]
    row_total, model_width = cand_ref.shape
    tiles = user_ref.shape[1]
    tile_rows = row_total // tiles
    items = kv_ref.shape[1]
    scale = width ** (-0.5)
    g, u = lax.axis_index("grp"), lax.axis_index("usr")
    n_z = n_usr // 2
    x, c = g // 2, g % 2
    z, y = u // 2, u % 2
    to_x = ((1 - x) * 2 + c, u)
    to_c = (x * 2 + (1 - c), u)
    to_y = (g, z * 2 + (1 - y))

    def slot_of(xx, cc, yy, zz):
        return (xx * 2 + cc) * n_usr + zz * 2 + yy

    def w_copy(slot, part, target, sem):
        half = depth // 2
        lo, size = (0, depth) if part is None else (part * half, half)
        view = w_all.at[slot, pl.ds(lo, size), :]
        return pltpu.make_async_remote_copy(
            src_ref=view,
            dst_ref=view,
            send_sem=w_send.at[sem],
            recv_sem=w_recv.at[slot, part or 0],
            device_id=target,
            device_id_type=MESH,
        )

    def o_copy(slot, part, target, sem):
        view = wo_all.at[slot]
        return pltpu.make_async_remote_copy(
            src_ref=view,
            dst_ref=view,
            send_sem=o_send.at[sem],
            recv_sem=o_recv.at[slot],
            device_id=target,
            device_id_type=MESH,
        )

    is_query, x_is_query = (x == 0) & (c == 0), (x == 1) & (c == 0)
    sib_is_query, diagonal_is_query = (x == 0) & (c == 1), (x == 1) & (c == 1)

    def along_z(slot, zz, base):
        up, down = (zz <= z) & (z + 1 < n_z), (zz >= z) & (z > 0)
        return [
            (up, slot, None, (g, (z + 1) * 2 + y), base),
            (down, slot, None, (g, (z - 1) * 2 + y), base + 1),
        ]

    def sends_own():
        me = slot_of(x, c, y, z)
        return along_z(me, z, 0) + [(None, me, None, to_y, 2), (None, me, None, to_c, 3)]

    def sends_across():
        return [(None, slot_of(x, c, y, z), None, to_x, 4)]

    def sends_line(zz):
        slot = slot_of(x, c, y, zz)
        base = 5 + zz * 5
        return along_z(slot, zz, base) + [
            (None, slot, None, to_x, base + 2),
            (None, slot, None, to_y, base + 3),
            (None, slot, None, to_c, base + 4),
        ]

    def sends_y(k):
        slot = slot_of(x, c, 1 - y, (z + k) % n_z)
        base = 5 + n_z * 5 + k * 2
        return [(None, slot, None, to_x, base), (None, slot, None, to_c, base + 1)]

    def sends_x(k):
        slot = slot_of(1 - x, c, y, (z + k) % n_z)
        return [(None, slot, None, to_c, 5 + n_z * 7 + k)]

    def sends_corner(k):
        slot = slot_of(1 - x, c, 1 - y, (z + k) % n_z)
        return [(None, slot, None, to_c, 5 + n_z * 8 + k)]

    def sends_query(zz, part):
        slot = slot_of(0, 0, y, zz)
        base = 5 + n_z * 9 + zz * 10 + part * 5
        up, down = (x == 0) & (zz <= z) & (z + 1 < n_z), (x == 0) & (zz >= z) & (z > 0)
        return [
            (up, slot, part, (g, (z + 1) * 2 + y), base),
            (down, slot, part, (g, (z - 1) * 2 + y), base + 1),
            (x == 0, slot, part, to_x, base + 2),
            (None, slot, part, to_y, base + 3),
            (None, slot, part, to_c, base + 4),
        ]

    def sends_query_y(k, part):
        slot = slot_of(0, 0, 1 - y, (z + k) % n_z)
        return [(None, slot, part, to_c, 5 + n_z * 19 + k * 2 + part)]

    early, late = x == 1, (x == 0) & (c == 1)

    def not_y(listed):
        return [entry for entry in listed if entry[3] is not to_y]

    def only_y(listed):
        return [entry for entry in listed if entry[3] is to_y]

    def each(copy, listed, act):
        for needed, slot, part, target, sem in listed:
            if needed is None:
                act(copy(slot, part, target, sem))
            else:
                pl.when(needed)(lambda a=(slot, part, target, sem): act(copy(*a)))

    def start(descriptor):
        descriptor.start()

    def sent(descriptor):
        descriptor.wait_send()

    def arrived(copy, slot, part):
        copy(slot, part, to_c, 0).wait_recv()

    def project(slot):
        block = silu(jnp.dot(normed[...], w_all[slot], preferred_element_type=jnp.float32))
        proj[slot] = block.astype(jnp.bfloat16).reshape(tiles, tile_rows, width)

    def relay(slot, listed, skip):
        @pl.when(jnp.logical_not(skip))
        def _():
            arrived(w_copy, slot, None)
            each(w_copy, listed, start)

        arrived(o_copy, slot, None)
        each(o_copy, listed, start)

        @pl.when(jnp.logical_not(skip))
        def _():
            project(slot)

    barrier = pltpu.get_barrier_semaphore()
    peers = [to_x, to_c] + [(g, (u + k) % n_usr) for k in range(1, n_usr)]
    for peer in peers:
        pl.semaphore_signal(barrier, inc=1, device_id=peer, device_id_type=MESH)
    mine = slot_of(x, c, y, z)
    loads = [
        pltpu.make_async_copy(cand_hbm, cand_ref, load_sem.at[0]),
        pltpu.make_async_copy(win_hbm, w_all.at[mine], load_sem.at[1]),
        pltpu.make_async_copy(wout_hbm, wo_all.at[mine], load_sem.at[2]),
        pltpu.make_async_copy(kv_hbm, kv_ref, load_sem.at[3]),
    ]
    for load in loads:
        load.start()
    loads[0].wait()
    normed[...] = norm_rows(cand_ref[...].astype(jnp.float32)).astype(jnp.bfloat16)
    loads[1].wait()
    pl.semaphore_wait(barrier, len(peers))

    @pl.when(early)
    def _():
        each(w_copy, sends_across() + not_y(sends_own()), start)

    def query_relay(zz, known):
        slot = slot_of(0, 0, y, zz)

        for part in range(2):

            @pl.when(jnp.logical_not(known))
            def _(part=part):
                arrived(w_copy, slot, part)

            @pl.when(c == 0)
            def _(part=part):
                each(w_copy, sends_query(zz, part), start)

    query_relay(z, is_query)
    project(slot_of(0, 0, y, z))

    def query_line(k, carry):
        for zz in (z - k, z + k):

            @pl.when((zz >= 0) & (zz < n_z))
            def _(zz=zz):
                query_relay(zz, False)
                project(slot_of(0, 0, y, zz))

            @pl.when((zz >= 0) & (zz < n_z) & early)
            def _(zz=zz):
                slot = slot_of(x, c, y, zz)
                arrived(w_copy, slot, None)
                each(w_copy, not_y(sends_line(zz)), start)
                project(slot)

        return carry

    lax.fori_loop(1, n_z, query_line, 0)

    def query_side(k, carry):
        slot = slot_of(0, 0, 1 - y, (z + k) % n_z)
        for part in range(2):
            arrived(w_copy, slot, part)

            @pl.when(c == 0)
            def _(part=part):
                each(w_copy, sends_query_y(k, part), start)

        project(slot)
        return carry

    lax.fori_loop(0, n_z, query_side, 0)

    def query_copy(k):
        holder = ((z + k // 2) % n_z) * 2 + (y + k) % 2
        return pltpu.make_async_remote_copy(
            src_ref=outgoing.at[holder],
            dst_ref=incoming.at[u],
            send_sem=q_send.at[k],
            recv_sem=q_recv.at[k],
            device_id=(g, holder),
            device_id_type=MESH,
        )

    def source_of(k):
        return ((z + n_z - k // 2) % n_z) * 2 + (y + k) % 2

    def answer_copy(k):
        source = source_of(k)
        return pltpu.make_async_remote_copy(
            src_ref=answers.at[source],
            dst_ref=returned.at[u],
            send_sem=a_send.at[k],
            recv_sem=a_recv.at[k],
            device_id=(g, source),
            device_id_type=MESH,
        )

    def tile_for(holder):
        chosen = 0
        for t in range(tiles):
            chosen = jnp.where(user_ref[0, t] == holder, t, chosen)
        return chosen

    def dispatch_step(k, carry):
        holder = ((z + k // 2) % n_z) * 2 + (y + k) % 2
        tile = tile_for(holder)
        for h in range(HEADS):
            outgoing[holder, h] = proj[h, tile]
        query_copy(k).start()
        return carry

    lax.fori_loop(1, n_usr, dispatch_step, 0)
    own_tile = tile_for(u)
    for h in range(HEADS):
        incoming[u, h] = proj[h, own_tile]

    positions = lax.broadcasted_iota(jnp.int32, (1, items), 1)
    kept = jnp.zeros((1, items), jnp.int32)
    for b in range(items // BLK):
        kept = jnp.where(positions // BLK == b, mask_ref[0, b], kept)
    live = jnp.where((positions < len_ref[0]) & (kept > 0), 1.0, 0.0)

    loads[3].wait()
    for h in range(HEADS):
        key_heads[h] = kv_ref[0, :, h * width : (h + 1) * width].T

    def attend(slot, dest):
        for h in range(HEADS):
            values = kv_ref[0, :, model_width + h * width : model_width + (h + 1) * width]
            scores = jnp.dot(incoming[slot, h], key_heads[h], preferred_element_type=jnp.float32)
            weights = (silu(scores * scale) * live).astype(jnp.bfloat16)
            dest[slot, h] = jnp.dot(weights, values, preferred_element_type=jnp.float32).astype(
                jnp.bfloat16
            )

    def answer(k):
        query_copy(k).wait_recv()
        attend(source_of(k), answers)
        answer_copy(k).start()

    @pl.when(late)
    def _():
        each(w_copy, sends_own() + sends_across(), start)

    @pl.when(early)
    def _():
        each(w_copy, only_y(sends_own()), start)

    def line_y(zz, carry):
        @pl.when(early & (zz != z))
        def _():
            each(w_copy, only_y(sends_line(zz)), start)

        return carry

    lax.fori_loop(0, n_z, line_y, 0)

    @pl.when(jnp.logical_not(is_query))
    def _():
        project(mine)

    loads[2].wait()
    each(o_copy, sends_own() + sends_across(), start)

    attend(u, returned)

    def line_step(k, carry):
        for zz in (z - k, z + k):

            @pl.when((zz >= 0) & (zz < n_z))
            def _(zz=zz):
                relay(slot_of(x, c, y, zz), sends_line(zz), jnp.logical_not(late))

        answer(k)
        return carry

    lax.fori_loop(1, n_z, line_step, 0)

    def side_step(k, carry):
        zz = (z + k) % n_z
        relay(slot_of(x, c, 1 - y, zz), sends_y(k), is_query)
        relay(slot_of(1 - x, c, y, zz), sends_x(k), x_is_query)
        relay(slot_of(x, 1 - c, y, zz), [], sib_is_query)
        answer(n_z + k)
        return carry

    lax.fori_loop(0, n_z, side_step, 0)

    def corner_step(k, carry):
        zz = (z + k) % n_z
        relay(slot_of(1 - x, c, 1 - y, zz), sends_corner(k), x_is_query)
        relay(slot_of(x, 1 - c, 1 - y, zz), [], sib_is_query)
        relay(slot_of(1 - x, 1 - c, y, zz), [], diagonal_is_query)
        return carry

    lax.fori_loop(0, n_z, corner_step, 0)

    def last_step(k, carry):
        slot = slot_of(1 - x, 1 - c, 1 - y, (z + k) % n_z)
        relay(slot, [], diagonal_is_query)
        return carry

    lax.fori_loop(0, n_z, last_step, 0)

    def own_step(h, carry):
        queries = proj[h].astype(jnp.float32)
        keys = proj[HEADS + h].astype(jnp.float32)
        strength = silu(jnp.sum(queries * keys, axis=-1, keepdims=True) * scale)
        own[h] = strength * proj[2 * HEADS + h].astype(jnp.float32)
        return carry

    lax.fori_loop(0, HEADS, own_step, 0)

    def return_step(k, carry):
        answer_copy(k).wait_recv()
        return carry

    lax.fori_loop(1, n_usr, return_step, 0)

    def tile_step(t, carry):
        holder = user_ref[0, t]
        combined = jnp.concatenate(
            [returned[holder, h].astype(jnp.float32) + own[h, t] for h in range(HEADS)], axis=-1
        )
        units = jnp.concatenate([proj[3 * HEADS + h, t] for h in range(HEADS)], axis=-1)
        gated[t] = (norm_rows(combined) * units.astype(jnp.float32)).astype(jnp.bfloat16)
        return carry

    lax.fori_loop(0, tiles, tile_step, 0)

    slots_here = lax.broadcasted_iota(jnp.int32, (tile_rows, 1), 0)
    for lo in range(0, model_width, 256):
        weights = wo_all[:, :, lo : lo + 256].reshape(model_width, 256)
        mixed = jnp.dot(
            gated[...].reshape(row_total, model_width), weights, preferred_element_type=jnp.float32
        )
        for t in range(tiles):
            rows = slice(t * tile_rows, (t + 1) * tile_rows)
            total = mixed[rows] + cand_ref[rows, lo : lo + 256].astype(jnp.float32)
            out_ref[rows, lo : lo + 256] = jnp.where(slots_here < count_ref[t], total, 0.0).astype(
                jnp.bfloat16
            )

    each(o_copy, sends_own() + sends_across(), sent)

    @pl.when(jnp.logical_not(is_query))
    def _():
        each(w_copy, sends_own() + sends_across(), sent)

    def sent_line(zz, carry):
        @pl.when(zz != z)
        def _():
            each(o_copy, sends_line(zz), sent)

        @pl.when((zz != z) & jnp.logical_not(is_query))
        def _():
            each(w_copy, sends_line(zz), sent)

        @pl.when(c == 0)
        def _():
            for part in range(2):
                each(w_copy, sends_query(zz, part) + sends_query_y(zz, part), sent)

        return carry

    def sent_rest(k, carry):
        by_y, by_x = sends_y(k), sends_x(k) + sends_corner(k)
        each(o_copy, by_y + by_x, sent)

        @pl.when(jnp.logical_not(is_query))
        def _():
            each(w_copy, by_y, sent)

        @pl.when(jnp.logical_not(x_is_query))
        def _():
            each(w_copy, by_x, sent)

        return carry

    def sent_exchange(k, carry):
        query_copy(k).wait_send()
        answer_copy(k).wait_send()
        return carry

    lax.fori_loop(0, n_z, sent_line, 0)
    lax.fori_loop(0, n_z, sent_rest, 0)
    lax.fori_loop(1, n_usr, sent_exchange, 0)


def fused_shards(
    candidates, hist_kv, hist_len, block_mask, tile_user, tile_count, weight_in, weight_out
):
    row_total, model_width = candidates.shape
    n_usr, n_grp = lax.axis_size("usr"), lax.axis_size("grp")
    devices = n_usr * n_grp
    depth, width = weight_in.shape
    out_rows = weight_out.shape[0]
    tiles = tile_user.shape[0]
    tile_rows = row_total // tiles
    sends = 5 + 21 * (n_usr // 2)
    exchange = pltpu.VMEM((n_usr, HEADS, tile_rows, width), jnp.bfloat16)
    dma = pltpu.SemaphoreType.DMA
    in_any = pl.BlockSpec(memory_space=pl.ANY)
    in_vmem = pl.BlockSpec(memory_space=pltpu.VMEM)
    in_smem = pl.BlockSpec(memory_space=pltpu.SMEM)
    flops = 2 * row_total * model_width * model_width * 5 + 8 * n_usr * tile_rows * hist_kv.shape[1] * model_width
    return pl.pallas_call(
        functools.partial(layer_kernel, n_usr),
        out_shape=jax.ShapeDtypeStruct((row_total, model_width), jnp.bfloat16),
        in_specs=[in_any, in_any, in_smem, in_smem, in_smem, in_smem, in_any, in_any],
        out_specs=in_vmem,
        scratch_shapes=[
            pltpu.VMEM((row_total, model_width), jnp.bfloat16),
            pltpu.VMEM(hist_kv.shape, jnp.bfloat16),
            pltpu.VMEM((HEADS, width, hist_kv.shape[1]), jnp.bfloat16),
            pltpu.VMEM((row_total, model_width), jnp.bfloat16),
            pltpu.VMEM((devices, depth, width), jnp.bfloat16),
            pltpu.VMEM((devices, out_rows, model_width), jnp.bfloat16),
            pltpu.VMEM((devices, tiles, tile_rows, width), jnp.bfloat16),
            pltpu.VMEM((HEADS, tiles, tile_rows, width), jnp.float32),
            exchange,
            exchange,
            exchange,
            exchange,
            pltpu.VMEM((tiles, tile_rows, model_width), jnp.bfloat16),
            dma((devices, 2)),
            dma((devices,)),
            dma((sends,)),
            dma((5 + 9 * (n_usr // 2),)),
            dma((n_usr,)),
            dma((n_usr,)),
            dma((n_usr,)),
            dma((n_usr,)),
            dma((4,)),
        ],
        compiler_params=pltpu.CompilerParams(
            collective_id=0, has_side_effects=True, vmem_limit_bytes=60 * 1024 * 1024
        ),
        cost_estimate=pl.CostEstimate(flops=flops, bytes_accessed=4 * 1024 * 1024, transcendentals=0),
    )(candidates, hist_kv, hist_len, block_mask, tile_user.T, tile_count, weight_in, weight_out)


def solution(mesh):
    in_specs = (
        P(("grp", "usr"), None),
        P(("grp", "usr"), None, None),
        P(("grp", "usr")),
        P(("grp", "usr"), None),
        P(("grp", "usr"), None),
        P(("grp", "usr")),
        P(None, ("grp", "usr")),
        P(("grp", "usr"), None),
    )
    out_specs = P(("grp", "usr"), None)
    fits = mesh.shape["grp"] == 4 and mesh.shape["usr"] == HEADS
    body = fused_shards if fits else shards
    return jax.shard_map(body, mesh=mesh, in_specs=in_specs, out_specs=out_specs, check_vma=False)
```

```python
import functools
import math

import jax
import jax.numpy as jnp
from jax import lax
from jax.experimental import pallas as pl
from jax.experimental.pallas import tpu as pltpu
from jax.sharding import PartitionSpec as P

HEADS = 8
BLK = 128
MESH = pl.DeviceIdType.MESH


def norm_rows(values_in):
    centred = values_in - jnp.mean(values_in, axis=-1, keepdims=True)
    variance = jnp.mean(centred * centred, axis=-1, keepdims=True)
    return centred * lax.rsqrt(variance + 1e-05)


def attend_rows(query_rows, hist_keys, hist_values, live_items, score_scale):
    row_total = query_rows.shape[0]
    model_width = query_rows.shape[1]
    head_dim = model_width // HEADS
    query_heads = query_rows.reshape(row_total, HEADS, head_dim)
    key_heads = hist_keys.reshape(-1, HEADS, head_dim)
    value_heads = hist_values.reshape(-1, HEADS, head_dim)
    scores = (
        jnp.einsum("nhd,lhd->hnl", query_heads, key_heads, preferred_element_type=jnp.float32)
        * score_scale
    )
    weights = (jax.nn.silu(scores) * live_items).astype(jnp.bfloat16)
    attended = jnp.einsum("hnl,lhd->nhd", weights, value_heads, preferred_element_type=jnp.float32)
    return attended.reshape(row_total, model_width)


def own_term(queries, self_keys, self_values, score_scale):
    row_total = queries.shape[0]
    products = (queries.astype(jnp.float32) * self_keys.astype(jnp.float32)).reshape(
        row_total, HEADS, -1
    )
    strength = jax.nn.silu(jnp.sum(products, axis=2) * score_scale)
    value_heads = self_values.astype(jnp.float32).reshape(row_total, HEADS, -1)
    return (strength[:, :, None] * value_heads).reshape(row_total, -1)


def holder_attend(incoming, hist_keys, hist_values, live_items, score_scale):
    slot_total, item_count, model_width = incoming.shape
    per_group = math.gcd(slot_total, max(1, 512 // item_count))
    group_total = slot_total // per_group

    def answer_rows(row_block):
        return attend_rows(row_block, hist_keys, hist_values, live_items, score_scale).astype(
            jnp.bfloat16
        )

    row_blocks = incoming.reshape(group_total, per_group * item_count, model_width)
    answered = lax.map(answer_rows, row_blocks)
    return answered.reshape(slot_total, item_count, model_width)


def shards(candidates, hist_kv, hist_len, block_mask, tile_user, tile_count, weight_in, weight_out):
    row_total, model_width = candidates.shape
    tiles_here = tile_user.shape[0]
    tile_rows = row_total // tiles_here
    score_scale = (model_width // HEADS) ** (-0.5)
    holders = lax.axis_size("usr")
    normed = norm_rows(candidates.astype(jnp.float32)).astype(jnp.bfloat16)
    projected = jax.nn.silu(
        jnp.dot(
            normed,
            lax.all_gather(weight_in, ("grp", "usr"), axis=1, tiled=True),
            preferred_element_type=jnp.float32,
        )
    ).astype(jnp.bfloat16)
    queries = projected[:, :model_width]
    self_keys = projected[:, model_width : 2 * model_width]
    self_values = projected[:, 2 * model_width : 3 * model_width]
    gate_units = projected[:, 3 * model_width :]
    own_part = own_term(queries, self_keys, self_values, score_scale)
    tile_dest = tile_user[:, 0]
    outgoing = jnp.zeros((holders, tile_rows, model_width), jnp.bfloat16)
    outgoing = outgoing.at[tile_dest].set(queries.reshape(tiles_here, tile_rows, model_width))
    hist_keys = hist_kv[0, :, :model_width]
    hist_values = hist_kv[0, :, model_width:]
    positions = jnp.arange(hist_kv.shape[1], dtype=jnp.int32)
    live_items = ((positions < hist_len[0]) & (jnp.repeat(block_mask[0], BLK) > 0)).astype(
        jnp.float32
    )
    incoming = lax.all_to_all(outgoing, "usr", split_axis=0, concat_axis=0, tiled=True)
    returned = lax.all_to_all(
        holder_attend(incoming, hist_keys, hist_values, live_items, score_scale),
        "usr",
        split_axis=0,
        concat_axis=0,
        tiled=True,
    )
    history = returned[tile_dest].reshape(row_total, model_width)
    combined = history.astype(jnp.float32) + own_part
    gated_rows = (norm_rows(combined) * gate_units.astype(jnp.float32)).astype(jnp.bfloat16)
    mixed_rows = jnp.dot(
        gated_rows,
        lax.all_gather(weight_out, ("grp", "usr"), axis=0, tiled=True),
        preferred_element_type=jnp.float32,
    )
    mixed_rows = mixed_rows + candidates.astype(jnp.float32)
    live_rows = (jnp.arange(tile_rows, dtype=jnp.int32)[None, :] < tile_count[:, None]).reshape(-1)
    return jnp.where(live_rows[:, None], mixed_rows, 0.0).astype(jnp.bfloat16)


def silu(v):
    half = 0.5 * v
    return half + half * jnp.tanh(half)


def layer_kernel(
    n_usr,
    cand_hbm,
    kv_hbm,
    len_ref,
    mask_ref,
    user_ref,
    count_ref,
    win_hbm,
    wout_hbm,
    out_ref,
    cand_ref,
    kv_ref,
    key_heads,
    normed,
    w_all,
    wo_all,
    proj,
    own,
    outgoing,
    incoming,
    answers,
    returned,
    gated,
    w_recv,
    o_recv,
    w_send,
    o_send,
    q_recv,
    q_send,
    a_recv,
    a_send,
    load_sem,
):
    depth, width = win_hbm.shape
    out_rows = wout_hbm.shape[0]
    row_total, model_width = cand_ref.shape
    tiles = user_ref.shape[1]
    tile_rows = row_total // tiles
    items = kv_ref.shape[1]
    scale = width ** (-0.5)
    g, u = lax.axis_index("grp"), lax.axis_index("usr")
    n_z = n_usr // 2
    x, c = g // 2, g % 2
    z, y = u // 2, u % 2
    to_x = ((1 - x) * 2 + c, u)
    to_c = (x * 2 + (1 - c), u)
    to_y = (g, z * 2 + (1 - y))

    def slot_of(xx, cc, yy, zz):
        return (xx * 2 + cc) * n_usr + zz * 2 + yy

    def w_copy(slot, part, target, sem):
        half = depth // 2
        lo, size = (0, depth) if part is None else (part * half, half)
        view = w_all.at[slot, pl.ds(lo, size), :]
        return pltpu.make_async_remote_copy(
            src_ref=view,
            dst_ref=view,
            send_sem=w_send.at[sem],
            recv_sem=w_recv.at[slot, part or 0],
            device_id=target,
            device_id_type=MESH,
        )

    def o_copy(slot, part, target, sem):
        view = wo_all.at[slot]
        return pltpu.make_async_remote_copy(
            src_ref=view,
            dst_ref=view,
            send_sem=o_send.at[sem],
            recv_sem=o_recv.at[slot],
            device_id=target,
            device_id_type=MESH,
        )

    is_query, x_is_query = (x == 0) & (c == 0), (x == 1) & (c == 0)
    sib_is_query, diagonal_is_query = (x == 0) & (c == 1), (x == 1) & (c == 1)

    def along_z(slot, zz, base):
        up, down = (zz <= z) & (z + 1 < n_z), (zz >= z) & (z > 0)
        return [
            (up, slot, None, (g, (z + 1) * 2 + y), base),
            (down, slot, None, (g, (z - 1) * 2 + y), base + 1),
        ]

    def sends_own():
        me = slot_of(x, c, y, z)
        return along_z(me, z, 0) + [(None, me, None, to_y, 2), (None, me, None, to_c, 3)]

    def sends_across():
        return [(None, slot_of(x, c, y, z), None, to_x, 4)]

    def sends_line(zz):
        slot = slot_of(x, c, y, zz)
        base = 5 + zz * 5
        return along_z(slot, zz, base) + [
            (None, slot, None, to_x, base + 2),
            (None, slot, None, to_y, base + 3),
            (None, slot, None, to_c, base + 4),
        ]

    def sends_y(k):
        slot = slot_of(x, c, 1 - y, (z + k) % n_z)
        base = 5 + n_z * 5 + k * 2
        return [(None, slot, None, to_x, base), (None, slot, None, to_c, base + 1)]

    def sends_x(k):
        slot = slot_of(1 - x, c, y, (z + k) % n_z)
        return [(None, slot, None, to_c, 5 + n_z * 7 + k)]

    def sends_corner(k):
        slot = slot_of(1 - x, c, 1 - y, (z + k) % n_z)
        return [(None, slot, None, to_c, 5 + n_z * 8 + k)]

    def sends_y_halves(k):
        whole, relayed = sends_y(k)
        return [(x == 0,) + whole[1:], (x == 1, whole[1], 0) + whole[3:], relayed]

    def sends_x_halves(k):
        slot = slot_of(1 - x, c, y, (z + k) % n_z)
        return sends_x(k) + [(x == 0, slot, 1, to_y, 5 + n_z * 21 + k)]

    def sends_corner_halves(k):
        slot, base = slot_of(1 - x, c, 1 - y, (z + k) % n_z), 5 + n_z * 8 + k
        return [
            (x == 1, slot, None, to_c, base),
            (x == 0, slot, 0, to_c, base),
            (x == 0, slot, 1, to_c, 5 + n_z * 22 + k),
        ]

    def sends_query(zz, part):
        slot = slot_of(0, 0, y, zz)
        base = 5 + n_z * 9 + zz * 10 + part * 5
        up, down = (x == 0) & (zz <= z) & (z + 1 < n_z), (x == 0) & (zz >= z) & (z > 0)
        return [
            (up, slot, part, (g, (z + 1) * 2 + y), base),
            (down, slot, part, (g, (z - 1) * 2 + y), base + 1),
            (x == 0, slot, part, to_x, base + 2),
            (None, slot, part, to_y, base + 3),
            (None, slot, part, to_c, base + 4),
        ]

    def sends_query_y(k, part):
        slot = slot_of(0, 0, 1 - y, (z + k) % n_z)
        return [(None, slot, part, to_c, 5 + n_z * 19 + k * 2 + part)]

    early, late = x == 1, (x == 0) & (c == 1)

    def not_y(listed):
        return [entry for entry in listed if entry[3] is not to_y]

    def only_y(listed):
        return [entry for entry in listed if entry[3] is to_y]

    def each(copy, listed, act):
        for needed, slot, part, target, sem in listed:
            if needed is None:
                act(copy(slot, part, target, sem))
            else:
                pl.when(needed)(lambda a=(slot, part, target, sem): act(copy(*a)))

    def start(descriptor):
        descriptor.start()

    def sent(descriptor):
        descriptor.wait_send()

    def arrived(copy, slot, part):
        copy(slot, part, to_c, 0).wait_recv()

    def project(slot):
        block = silu(jnp.dot(normed[...], w_all[slot], preferred_element_type=jnp.float32))
        proj[slot] = block.astype(jnp.bfloat16).reshape(tiles, tile_rows, width)

    def relay(slot, listed, skip, halves=None, w_listed=None):
        w_listed = listed if w_listed is None else w_listed
        if halves is None:

            @pl.when(jnp.logical_not(skip))
            def _():
                arrived(w_copy, slot, None)
                each(w_copy, w_listed, start)
        else:

            @pl.when(jnp.logical_not(skip) & halves)
            def _():
                for part in range(2):
                    arrived(w_copy, slot, part)
                    each(w_copy, [entry for entry in w_listed if entry[2] == part], start)

            @pl.when(jnp.logical_not(skip | halves))
            def _():
                arrived(w_copy, slot, None)
                each(w_copy, [entry for entry in w_listed if entry[2] is None], start)

        arrived(o_copy, slot, None)
        each(o_copy, listed, start)

        @pl.when(jnp.logical_not(skip))
        def _():
            project(slot)

    barrier = pltpu.get_barrier_semaphore()
    peers = [to_x, to_c] + [(g, (u + k) % n_usr) for k in range(1, n_usr)]
    for peer in peers:
        pl.semaphore_signal(barrier, inc=1, device_id=peer, device_id_type=MESH)
    mine = slot_of(x, c, y, z)
    loads = [
        pltpu.make_async_copy(cand_hbm, cand_ref, load_sem.at[0]),
        pltpu.make_async_copy(win_hbm, w_all.at[mine], load_sem.at[1]),
        pltpu.make_async_copy(wout_hbm, wo_all.at[mine], load_sem.at[2]),
        pltpu.make_async_copy(kv_hbm, kv_ref, load_sem.at[3]),
    ]
    for load in loads:
        load.start()
    loads[0].wait()
    normed[...] = norm_rows(cand_ref[...].astype(jnp.float32)).astype(jnp.bfloat16)
    loads[1].wait()
    pl.semaphore_wait(barrier, len(peers))

    @pl.when(early)
    def _():
        each(w_copy, sends_across() + not_y(sends_own()), start)

    def query_relay(zz, known):
        slot = slot_of(0, 0, y, zz)

        for part in range(2):

            @pl.when(jnp.logical_not(known))
            def _(part=part):
                arrived(w_copy, slot, part)

            @pl.when(c == 0)
            def _(part=part):
                each(w_copy, sends_query(zz, part), start)

    query_relay(z, is_query)
    project(slot_of(0, 0, y, z))

    def query_line(k, carry):
        for zz in (z - k, z + k):

            @pl.when((zz >= 0) & (zz < n_z))
            def _(zz=zz):
                query_relay(zz, False)
                project(slot_of(0, 0, y, zz))

            @pl.when((zz >= 0) & (zz < n_z) & early)
            def _(zz=zz):
                slot = slot_of(x, c, y, zz)
                arrived(w_copy, slot, None)
                each(w_copy, not_y(sends_line(zz)), start)
                project(slot)

        return carry

    lax.fori_loop(1, n_z, query_line, 0)

    def query_side(k, carry):
        slot = slot_of(0, 0, 1 - y, (z + k) % n_z)
        for part in range(2):
            arrived(w_copy, slot, part)

            @pl.when(c == 0)
            def _(part=part):
                each(w_copy, sends_query_y(k, part), start)

        project(slot)
        return carry

    lax.fori_loop(0, n_z, query_side, 0)

    def query_copy(k):
        holder = ((z + k // 2) % n_z) * 2 + (y + k) % 2
        return pltpu.make_async_remote_copy(
            src_ref=outgoing.at[holder],
            dst_ref=incoming.at[u],
            send_sem=q_send.at[k],
            recv_sem=q_recv.at[k],
            device_id=(g, holder),
            device_id_type=MESH,
        )

    def source_of(k):
        return ((z + n_z - k // 2) % n_z) * 2 + (y + k) % 2

    def answer_copy(k):
        source = source_of(k)
        return pltpu.make_async_remote_copy(
            src_ref=answers.at[source],
            dst_ref=returned.at[u],
            send_sem=a_send.at[k],
            recv_sem=a_recv.at[k],
            device_id=(g, source),
            device_id_type=MESH,
        )

    def tile_for(holder):
        chosen = 0
        for t in range(tiles):
            chosen = jnp.where(user_ref[0, t] == holder, t, chosen)
        return chosen

    def dispatch_step(k, carry):
        holder = ((z + k // 2) % n_z) * 2 + (y + k) % 2
        tile = tile_for(holder)
        for h in range(HEADS):
            outgoing[holder, h] = proj[h, tile]
        query_copy(k).start()
        return carry

    lax.fori_loop(1, n_usr, dispatch_step, 0)
    own_tile = tile_for(u)
    for h in range(HEADS):
        incoming[u, h] = proj[h, own_tile]

    positions = lax.broadcasted_iota(jnp.int32, (1, items), 1)
    kept = jnp.zeros((1, items), jnp.int32)
    for b in range(items // BLK):
        kept = jnp.where(positions // BLK == b, mask_ref[0, b], kept)
    live = jnp.where((positions < len_ref[0]) & (kept > 0), 1.0, 0.0)

    loads[3].wait()
    for h in range(HEADS):
        key_heads[h] = kv_ref[0, :, h * width : (h + 1) * width].T

    def attend(slot, dest):
        for h in range(HEADS):
            values = kv_ref[0, :, model_width + h * width : model_width + (h + 1) * width]
            scores = jnp.dot(incoming[slot, h], key_heads[h], preferred_element_type=jnp.float32)
            weights = (silu(scores * scale) * live).astype(jnp.bfloat16)
            dest[slot, h] = jnp.dot(weights, values, preferred_element_type=jnp.float32).astype(
                jnp.bfloat16
            )

    def answer(k):
        query_copy(k).wait_recv()
        attend(source_of(k), answers)
        answer_copy(k).start()

    @pl.when(late)
    def _():
        each(w_copy, sends_own() + sends_across(), start)

    @pl.when(early)
    def _():
        each(w_copy, only_y(sends_own()), start)

    def line_y(zz, carry):
        @pl.when(early & (zz != z))
        def _():
            each(w_copy, only_y(sends_line(zz)), start)

        return carry

    lax.fori_loop(0, n_z, line_y, 0)

    @pl.when(jnp.logical_not(is_query))
    def _():
        project(mine)

    loads[2].wait()
    each(o_copy, sends_own() + sends_across(), start)

    attend(u, returned)

    def line_step(k, carry):
        for zz in (z - k, z + k):

            @pl.when((zz >= 0) & (zz < n_z))
            def _(zz=zz):
                relay(slot_of(x, c, y, zz), sends_line(zz), jnp.logical_not(late))

        answer(k)
        return carry

    lax.fori_loop(1, n_z, line_step, 0)

    def side_step(k, carry):
        zz = (z + k) % n_z
        relay(slot_of(x, c, 1 - y, zz), sends_y(k), is_query, None, sends_y_halves(k))
        relay(slot_of(1 - x, c, y, zz), sends_x(k), x_is_query, None, sends_x_halves(k))
        relay(slot_of(x, 1 - c, y, zz), [], sib_is_query)
        answer(n_z + k)
        return carry

    lax.fori_loop(0, n_z, side_step, 0)

    def corner_step(k, carry):
        zz = (z + k) % n_z
        relay(slot_of(1 - x, c, 1 - y, zz), sends_corner(k), x_is_query, x == 0, sends_corner_halves(k))
        relay(slot_of(x, 1 - c, 1 - y, zz), [], sib_is_query)
        relay(slot_of(1 - x, 1 - c, y, zz), [], diagonal_is_query)
        return carry

    lax.fori_loop(0, n_z, corner_step, 0)

    def last_step(k, carry):
        slot = slot_of(1 - x, 1 - c, 1 - y, (z + k) % n_z)
        relay(slot, [], diagonal_is_query, x == 0)
        return carry

    lax.fori_loop(0, n_z, last_step, 0)

    def own_step(h, carry):
        queries = proj[h].astype(jnp.float32)
        keys = proj[HEADS + h].astype(jnp.float32)
        strength = silu(jnp.sum(queries * keys, axis=-1, keepdims=True) * scale)
        own[h] = strength * proj[2 * HEADS + h].astype(jnp.float32)
        return carry

    lax.fori_loop(0, HEADS, own_step, 0)

    def return_step(k, carry):
        answer_copy(k).wait_recv()
        return carry

    lax.fori_loop(1, n_usr, return_step, 0)

    def tile_step(t, carry):
        holder = user_ref[0, t]
        combined = jnp.concatenate(
            [returned[holder, h].astype(jnp.float32) + own[h, t] for h in range(HEADS)], axis=-1
        )
        units = jnp.concatenate([proj[3 * HEADS + h, t] for h in range(HEADS)], axis=-1)
        gated[t] = (norm_rows(combined) * units.astype(jnp.float32)).astype(jnp.bfloat16)
        return carry

    lax.fori_loop(0, tiles, tile_step, 0)

    slots_here = lax.broadcasted_iota(jnp.int32, (tile_rows, 1), 0)
    for lo in range(0, model_width, 256):
        weights = wo_all[:, :, lo : lo + 256].reshape(model_width, 256)
        mixed = jnp.dot(
            gated[...].reshape(row_total, model_width), weights, preferred_element_type=jnp.float32
        )
        for t in range(tiles):
            rows = slice(t * tile_rows, (t + 1) * tile_rows)
            total = mixed[rows] + cand_ref[rows, lo : lo + 256].astype(jnp.float32)
            out_ref[rows, lo : lo + 256] = jnp.where(slots_here < count_ref[t], total, 0.0).astype(
                jnp.bfloat16
            )

    each(o_copy, sends_own() + sends_across(), sent)

    @pl.when(jnp.logical_not(is_query))
    def _():
        each(w_copy, sends_own() + sends_across(), sent)

    def sent_line(zz, carry):
        @pl.when(zz != z)
        def _():
            each(o_copy, sends_line(zz), sent)

        @pl.when((zz != z) & jnp.logical_not(is_query))
        def _():
            each(w_copy, sends_line(zz), sent)

        @pl.when(c == 0)
        def _():
            for part in range(2):
                each(w_copy, sends_query(zz, part) + sends_query_y(zz, part), sent)

        return carry

    def sent_rest(k, carry):
        by_y, by_x = sends_y_halves(k), sends_x_halves(k) + sends_corner_halves(k)
        each(o_copy, sends_y(k) + sends_x(k) + sends_corner(k), sent)

        @pl.when(jnp.logical_not(is_query))
        def _():
            each(w_copy, by_y, sent)

        @pl.when(jnp.logical_not(x_is_query))
        def _():
            each(w_copy, by_x, sent)

        return carry

    def sent_exchange(k, carry):
        query_copy(k).wait_send()
        answer_copy(k).wait_send()
        return carry

    lax.fori_loop(0, n_z, sent_line, 0)
    lax.fori_loop(0, n_z, sent_rest, 0)
    lax.fori_loop(1, n_usr, sent_exchange, 0)


def fused_shards(
    candidates, hist_kv, hist_len, block_mask, tile_user, tile_count, weight_in, weight_out
):
    row_total, model_width = candidates.shape
    n_usr, n_grp = lax.axis_size("usr"), lax.axis_size("grp")
    devices = n_usr * n_grp
    depth, width = weight_in.shape
    out_rows = weight_out.shape[0]
    tiles = tile_user.shape[0]
    tile_rows = row_total // tiles
    sends = 5 + 23 * (n_usr // 2)
    exchange = pltpu.VMEM((n_usr, HEADS, tile_rows, width), jnp.bfloat16)
    dma = pltpu.SemaphoreType.DMA
    in_any = pl.BlockSpec(memory_space=pl.ANY)
    in_vmem = pl.BlockSpec(memory_space=pltpu.VMEM)
    in_smem = pl.BlockSpec(memory_space=pltpu.SMEM)
    flops = 2 * row_total * model_width * model_width * 5 + 8 * n_usr * tile_rows * hist_kv.shape[1] * model_width
    return pl.pallas_call(
        functools.partial(layer_kernel, n_usr),
        out_shape=jax.ShapeDtypeStruct((row_total, model_width), jnp.bfloat16),
        in_specs=[in_any, in_any, in_smem, in_smem, in_smem, in_smem, in_any, in_any],
        out_specs=in_vmem,
        scratch_shapes=[
            pltpu.VMEM((row_total, model_width), jnp.bfloat16),
            pltpu.VMEM(hist_kv.shape, jnp.bfloat16),
            pltpu.VMEM((HEADS, width, hist_kv.shape[1]), jnp.bfloat16),
            pltpu.VMEM((row_total, model_width), jnp.bfloat16),
            pltpu.VMEM((devices, depth, width), jnp.bfloat16),
            pltpu.VMEM((devices, out_rows, model_width), jnp.bfloat16),
            pltpu.VMEM((devices, tiles, tile_rows, width), jnp.bfloat16),
            pltpu.VMEM((HEADS, tiles, tile_rows, width), jnp.float32),
            exchange,
            exchange,
            exchange,
            exchange,
            pltpu.VMEM((tiles, tile_rows, model_width), jnp.bfloat16),
            dma((devices, 2)),
            dma((devices,)),
            dma((sends,)),
            dma((5 + 9 * (n_usr // 2),)),
            dma((n_usr,)),
            dma((n_usr,)),
            dma((n_usr,)),
            dma((n_usr,)),
            dma((4,)),
        ],
        compiler_params=pltpu.CompilerParams(
            collective_id=0, has_side_effects=True, vmem_limit_bytes=60 * 1024 * 1024
        ),
        cost_estimate=pl.CostEstimate(flops=flops, bytes_accessed=4 * 1024 * 1024, transcendentals=0),
    )(candidates, hist_kv, hist_len, block_mask, tile_user.T, tile_count, weight_in, weight_out)


def solution(mesh):
    in_specs = (
        P(("grp", "usr"), None),
        P(("grp", "usr"), None, None),
        P(("grp", "usr")),
        P(("grp", "usr"), None),
        P(("grp", "usr"), None),
        P(("grp", "usr")),
        P(None, ("grp", "usr")),
        P(("grp", "usr"), None),
    )
    out_specs = P(("grp", "usr"), None)
    fits = mesh.shape["grp"] == 4 and mesh.shape["usr"] == HEADS
    body = fused_shards if fits else shards
    return jax.shard_map(body, mesh=mesh, in_specs=in_specs, out_specs=out_specs, check_vma=False)
```

```python
import functools
import math

import jax
import jax.numpy as jnp
from jax import lax
from jax.experimental import pallas as pl
from jax.experimental.pallas import tpu as pltpu
from jax.sharding import PartitionSpec as P

HEADS = 8
BLK = 128
MESH = pl.DeviceIdType.MESH


def norm_rows(values_in):
    centred = values_in - jnp.mean(values_in, axis=-1, keepdims=True)
    variance = jnp.mean(centred * centred, axis=-1, keepdims=True)
    return centred * lax.rsqrt(variance + 1e-05)


def attend_rows(query_rows, hist_keys, hist_values, live_items, score_scale):
    row_total = query_rows.shape[0]
    model_width = query_rows.shape[1]
    head_dim = model_width // HEADS
    query_heads = query_rows.reshape(row_total, HEADS, head_dim)
    key_heads = hist_keys.reshape(-1, HEADS, head_dim)
    value_heads = hist_values.reshape(-1, HEADS, head_dim)
    scores = (
        jnp.einsum("nhd,lhd->hnl", query_heads, key_heads, preferred_element_type=jnp.float32)
        * score_scale
    )
    weights = (jax.nn.silu(scores) * live_items).astype(jnp.bfloat16)
    attended = jnp.einsum("hnl,lhd->nhd", weights, value_heads, preferred_element_type=jnp.float32)
    return attended.reshape(row_total, model_width)


def own_term(queries, self_keys, self_values, score_scale):
    row_total = queries.shape[0]
    products = (queries.astype(jnp.float32) * self_keys.astype(jnp.float32)).reshape(
        row_total, HEADS, -1
    )
    strength = jax.nn.silu(jnp.sum(products, axis=2) * score_scale)
    value_heads = self_values.astype(jnp.float32).reshape(row_total, HEADS, -1)
    return (strength[:, :, None] * value_heads).reshape(row_total, -1)


def holder_attend(incoming, hist_keys, hist_values, live_items, score_scale):
    slot_total, item_count, model_width = incoming.shape
    per_group = math.gcd(slot_total, max(1, 512 // item_count))
    group_total = slot_total // per_group

    def answer_rows(row_block):
        return attend_rows(row_block, hist_keys, hist_values, live_items, score_scale).astype(
            jnp.bfloat16
        )

    row_blocks = incoming.reshape(group_total, per_group * item_count, model_width)
    answered = lax.map(answer_rows, row_blocks)
    return answered.reshape(slot_total, item_count, model_width)


def shards(candidates, hist_kv, hist_len, block_mask, tile_user, tile_count, weight_in, weight_out):
    row_total, model_width = candidates.shape
    tiles_here = tile_user.shape[0]
    tile_rows = row_total // tiles_here
    score_scale = (model_width // HEADS) ** (-0.5)
    holders = lax.axis_size("usr")
    normed = norm_rows(candidates.astype(jnp.float32)).astype(jnp.bfloat16)
    projected = jax.nn.silu(
        jnp.dot(
            normed,
            lax.all_gather(weight_in, ("grp", "usr"), axis=1, tiled=True),
            preferred_element_type=jnp.float32,
        )
    ).astype(jnp.bfloat16)
    queries = projected[:, :model_width]
    self_keys = projected[:, model_width : 2 * model_width]
    self_values = projected[:, 2 * model_width : 3 * model_width]
    gate_units = projected[:, 3 * model_width :]
    own_part = own_term(queries, self_keys, self_values, score_scale)
    tile_dest = tile_user[:, 0]
    outgoing = jnp.zeros((holders, tile_rows, model_width), jnp.bfloat16)
    outgoing = outgoing.at[tile_dest].set(queries.reshape(tiles_here, tile_rows, model_width))
    hist_keys = hist_kv[0, :, :model_width]
    hist_values = hist_kv[0, :, model_width:]
    positions = jnp.arange(hist_kv.shape[1], dtype=jnp.int32)
    live_items = ((positions < hist_len[0]) & (jnp.repeat(block_mask[0], BLK) > 0)).astype(
        jnp.float32
    )
    incoming = lax.all_to_all(outgoing, "usr", split_axis=0, concat_axis=0, tiled=True)
    returned = lax.all_to_all(
        holder_attend(incoming, hist_keys, hist_values, live_items, score_scale),
        "usr",
        split_axis=0,
        concat_axis=0,
        tiled=True,
    )
    history = returned[tile_dest].reshape(row_total, model_width)
    combined = history.astype(jnp.float32) + own_part
    gated_rows = (norm_rows(combined) * gate_units.astype(jnp.float32)).astype(jnp.bfloat16)
    mixed_rows = jnp.dot(
        gated_rows,
        lax.all_gather(weight_out, ("grp", "usr"), axis=0, tiled=True),
        preferred_element_type=jnp.float32,
    )
    mixed_rows = mixed_rows + candidates.astype(jnp.float32)
    live_rows = (jnp.arange(tile_rows, dtype=jnp.int32)[None, :] < tile_count[:, None]).reshape(-1)
    return jnp.where(live_rows[:, None], mixed_rows, 0.0).astype(jnp.bfloat16)


def silu(v):
    half = 0.5 * v
    return half + half * jnp.tanh(half)


def layer_kernel(
    n_usr,
    cand_hbm,
    kv_hbm,
    len_ref,
    mask_ref,
    user_ref,
    count_ref,
    win_hbm,
    wout_hbm,
    out_ref,
    cand_ref,
    kv_ref,
    key_heads,
    normed,
    w_all,
    wo_all,
    proj,
    own,
    outgoing,
    incoming,
    answers,
    returned,
    gated,
    w_recv,
    o_recv,
    w_send,
    o_send,
    q_recv,
    q_send,
    a_recv,
    a_send,
    load_sem,
):
    depth, width = win_hbm.shape
    out_rows = wout_hbm.shape[0]
    row_total, model_width = cand_ref.shape
    tiles = user_ref.shape[1]
    tile_rows = row_total // tiles
    items = kv_ref.shape[1]
    scale = width ** (-0.5)
    g, u = lax.axis_index("grp"), lax.axis_index("usr")
    n_z = n_usr // 2
    x, c = g // 2, g % 2
    z, y = u // 2, u % 2
    to_x = ((1 - x) * 2 + c, u)
    to_c = (x * 2 + (1 - c), u)
    to_y = (g, z * 2 + (1 - y))

    def slot_of(xx, cc, yy, zz):
        return (xx * 2 + cc) * n_usr + zz * 2 + yy

    def w_copy(slot, part, target, sem):
        half = depth // 2
        lo, size = (0, depth) if part is None else (part * half, half)
        view = w_all.at[slot, pl.ds(lo, size), :]
        return pltpu.make_async_remote_copy(
            src_ref=view,
            dst_ref=view,
            send_sem=w_send.at[sem],
            recv_sem=w_recv.at[slot, part or 0],
            device_id=target,
            device_id_type=MESH,
        )

    def o_copy(slot, part, target, sem):
        view = wo_all.at[slot]
        return pltpu.make_async_remote_copy(
            src_ref=view,
            dst_ref=view,
            send_sem=o_send.at[sem],
            recv_sem=o_recv.at[slot],
            device_id=target,
            device_id_type=MESH,
        )

    is_query, x_is_query = (x == 0) & (c == 0), (x == 1) & (c == 0)
    sib_is_query, diagonal_is_query = (x == 0) & (c == 1), (x == 1) & (c == 1)

    def along_z(slot, zz, base):
        up, down = (zz <= z) & (z + 1 < n_z), (zz >= z) & (z > 0)
        return [
            (up, slot, None, (g, (z + 1) * 2 + y), base),
            (down, slot, None, (g, (z - 1) * 2 + y), base + 1),
        ]

    def sends_own():
        me = slot_of(x, c, y, z)
        return along_z(me, z, 0) + [(None, me, None, to_y, 2), (None, me, None, to_c, 3)]

    def sends_across():
        return [(None, slot_of(x, c, y, z), None, to_x, 4)]

    def sends_line(zz):
        slot = slot_of(x, c, y, zz)
        base = 5 + zz * 5
        return along_z(slot, zz, base) + [
            (None, slot, None, to_x, base + 2),
            (None, slot, None, to_y, base + 3),
            (None, slot, None, to_c, base + 4),
        ]

    def sends_y(k):
        slot = slot_of(x, c, 1 - y, (z + k) % n_z)
        base = 5 + n_z * 5 + k * 2
        return [(None, slot, None, to_x, base), (None, slot, None, to_c, base + 1)]

    def sends_x(k):
        slot = slot_of(1 - x, c, y, (z + k) % n_z)
        return [(None, slot, None, to_c, 5 + n_z * 7 + k)]

    def sends_corner(k):
        slot = slot_of(1 - x, c, 1 - y, (z + k) % n_z)
        return [(None, slot, None, to_c, 5 + n_z * 8 + k)]

    def sends_y_halves(k):
        whole, relayed = sends_y(k)
        return [(x == 0,) + whole[1:], (x == 1, whole[1], 0) + whole[3:], relayed]

    def sends_x_halves(k):
        slot = slot_of(1 - x, c, y, (z + k) % n_z)
        return sends_x(k) + [(x == 0, slot, 1, to_y, 5 + n_z * 21 + k)]

    def sends_corner_halves(k):
        slot, base = slot_of(1 - x, c, 1 - y, (z + k) % n_z), 5 + n_z * 8 + k
        return [
            (x == 1, slot, None, to_c, base),
            (x == 0, slot, 0, to_c, base),
            (x == 0, slot, 1, to_c, 5 + n_z * 22 + k),
        ]

    def sends_query(zz, part):
        slot = slot_of(0, 0, y, zz)
        base = 5 + n_z * 9 + zz * 10 + part * 5
        up, down = (x == 0) & (zz <= z) & (z + 1 < n_z), (x == 0) & (zz >= z) & (z > 0)
        return [
            (up, slot, part, (g, (z + 1) * 2 + y), base),
            (down, slot, part, (g, (z - 1) * 2 + y), base + 1),
            (x == 0, slot, part, to_x, base + 2),
            (None, slot, part, to_y, base + 3),
            (None, slot, part, to_c, base + 4),
        ]

    def sends_query_y(k, part):
        slot = slot_of(0, 0, 1 - y, (z + k) % n_z)
        return [(None, slot, part, to_c, 5 + n_z * 19 + k * 2 + part)]

    early, late = jnp.logical_not(is_query), (x == 0) & (c == 1)

    def not_y(listed):
        return [entry for entry in listed if entry[3] is not to_y]

    def only_y(listed):
        return [entry for entry in listed if entry[3] is to_y]

    def each(copy, listed, act):
        for needed, slot, part, target, sem in listed:
            if needed is None:
                act(copy(slot, part, target, sem))
            else:
                pl.when(needed)(lambda a=(slot, part, target, sem): act(copy(*a)))

    def start(descriptor):
        descriptor.start()

    def sent(descriptor):
        descriptor.wait_send()

    def arrived(copy, slot, part):
        copy(slot, part, to_c, 0).wait_recv()

    def project(slot):
        block = silu(jnp.dot(normed[...], w_all[slot], preferred_element_type=jnp.float32))
        proj[slot] = block.astype(jnp.bfloat16).reshape(tiles, tile_rows, width)

    def relay(slot, listed, skip, halves=None, w_listed=None):
        w_listed = listed if w_listed is None else w_listed
        if halves is None:

            @pl.when(jnp.logical_not(skip))
            def _():
                arrived(w_copy, slot, None)
                each(w_copy, w_listed, start)
        else:

            @pl.when(jnp.logical_not(skip) & halves)
            def _():
                for part in range(2):
                    arrived(w_copy, slot, part)
                    each(w_copy, [entry for entry in w_listed if entry[2] == part], start)

            @pl.when(jnp.logical_not(skip | halves))
            def _():
                arrived(w_copy, slot, None)
                each(w_copy, [entry for entry in w_listed if entry[2] is None], start)

        arrived(o_copy, slot, None)
        each(o_copy, listed, start)

        @pl.when(jnp.logical_not(skip))
        def _():
            project(slot)

    barrier = pltpu.get_barrier_semaphore()
    peers = [to_x, to_c] + [(g, (u + k) % n_usr) for k in range(1, n_usr)]
    for peer in peers:
        pl.semaphore_signal(barrier, inc=1, device_id=peer, device_id_type=MESH)
    mine = slot_of(x, c, y, z)
    loads = [
        pltpu.make_async_copy(cand_hbm, cand_ref, load_sem.at[0]),
        pltpu.make_async_copy(win_hbm, w_all.at[mine], load_sem.at[1]),
        pltpu.make_async_copy(wout_hbm, wo_all.at[mine], load_sem.at[2]),
        pltpu.make_async_copy(kv_hbm, kv_ref, load_sem.at[3]),
    ]
    for load in loads:
        load.start()
    loads[0].wait()
    normed[...] = norm_rows(cand_ref[...].astype(jnp.float32)).astype(jnp.bfloat16)
    loads[1].wait()
    pl.semaphore_wait(barrier, len(peers))

    @pl.when(x == 1)
    def _():
        each(w_copy, sends_across() + not_y(sends_own()), start)

    def query_relay(zz, known):
        slot = slot_of(0, 0, y, zz)

        for part in range(2):

            @pl.when(jnp.logical_not(known))
            def _(part=part):
                arrived(w_copy, slot, part)

            @pl.when(c == 0)
            def _(part=part):
                each(w_copy, sends_query(zz, part), start)

    query_relay(z, is_query)

    @pl.when(late)
    def _():
        each(w_copy, sends_across() + not_y(sends_own()), start)

    project(slot_of(0, 0, y, z))

    def query_line(k, carry):
        for zz in (z - k, z + k):

            @pl.when((zz >= 0) & (zz < n_z))
            def _(zz=zz):
                query_relay(zz, False)
                project(slot_of(0, 0, y, zz))

            @pl.when((zz >= 0) & (zz < n_z) & early)
            def _(zz=zz):
                slot = slot_of(x, c, y, zz)
                arrived(w_copy, slot, None)
                each(w_copy, not_y(sends_line(zz)), start)
                project(slot)

        return carry

    lax.fori_loop(1, n_z, query_line, 0)

    def query_side(k, carry):
        slot = slot_of(0, 0, 1 - y, (z + k) % n_z)
        for part in range(2):
            arrived(w_copy, slot, part)

            @pl.when(c == 0)
            def _(part=part):
                each(w_copy, sends_query_y(k, part), start)

        project(slot)
        return carry

    lax.fori_loop(0, n_z, query_side, 0)

    def query_copy(k):
        holder = ((z + k // 2) % n_z) * 2 + (y + k) % 2
        return pltpu.make_async_remote_copy(
            src_ref=outgoing.at[holder],
            dst_ref=incoming.at[u],
            send_sem=q_send.at[k],
            recv_sem=q_recv.at[k],
            device_id=(g, holder),
            device_id_type=MESH,
        )

    def source_of(k):
        return ((z + n_z - k // 2) % n_z) * 2 + (y + k) % 2

    def answer_copy(k):
        source = source_of(k)
        return pltpu.make_async_remote_copy(
            src_ref=answers.at[source],
            dst_ref=returned.at[u],
            send_sem=a_send.at[k],
            recv_sem=a_recv.at[k],
            device_id=(g, source),
            device_id_type=MESH,
        )

    def tile_for(holder):
        chosen = 0
        for t in range(tiles):
            chosen = jnp.where(user_ref[0, t] == holder, t, chosen)
        return chosen

    def dispatch_step(k, carry):
        holder = ((z + k // 2) % n_z) * 2 + (y + k) % 2
        tile = tile_for(holder)
        for h in range(HEADS):
            outgoing[holder, h] = proj[h, tile]
        query_copy(k).start()
        return carry

    lax.fori_loop(1, n_usr, dispatch_step, 0)
    own_tile = tile_for(u)
    for h in range(HEADS):
        incoming[u, h] = proj[h, own_tile]

    positions = lax.broadcasted_iota(jnp.int32, (1, items), 1)
    kept = jnp.zeros((1, items), jnp.int32)
    for b in range(items // BLK):
        kept = jnp.where(positions // BLK == b, mask_ref[0, b], kept)
    live = jnp.where((positions < len_ref[0]) & (kept > 0), 1.0, 0.0)

    loads[3].wait()
    for h in range(HEADS):
        key_heads[h] = kv_ref[0, :, h * width : (h + 1) * width].T

    def attend(slot, dest):
        for h in range(HEADS):
            values = kv_ref[0, :, model_width + h * width : model_width + (h + 1) * width]
            scores = jnp.dot(incoming[slot, h], key_heads[h], preferred_element_type=jnp.float32)
            weights = (silu(scores * scale) * live).astype(jnp.bfloat16)
            dest[slot, h] = jnp.dot(weights, values, preferred_element_type=jnp.float32).astype(
                jnp.bfloat16
            )

    def answer(k):
        query_copy(k).wait_recv()
        attend(source_of(k), answers)
        answer_copy(k).start()

    @pl.when(early)
    def _():
        each(w_copy, only_y(sends_own()), start)

    def line_y(zz, carry):
        @pl.when(early & (zz != z))
        def _():
            each(w_copy, only_y(sends_line(zz)), start)

        return carry

    lax.fori_loop(0, n_z, line_y, 0)

    @pl.when(jnp.logical_not(is_query))
    def _():
        project(mine)

    loads[2].wait()
    each(o_copy, sends_own() + sends_across(), start)

    attend(u, returned)

    def line_step(k, carry):
        answer(k)
        for zz in (z - k, z + k):

            @pl.when((zz >= 0) & (zz < n_z))
            def _(zz=zz):
                arrived(o_copy, slot_of(x, c, y, zz), None)
                each(o_copy, sends_line(zz), start)

        return carry

    lax.fori_loop(1, n_z, line_step, 0)

    def side_step(k, carry):
        zz = (z + k) % n_z
        relay(slot_of(x, c, 1 - y, zz), sends_y(k), is_query, None, sends_y_halves(k))
        relay(slot_of(1 - x, c, y, zz), sends_x(k), x_is_query, None, sends_x_halves(k))
        relay(slot_of(x, 1 - c, y, zz), [], sib_is_query)
        answer(n_z + k)
        return carry

    lax.fori_loop(0, n_z, side_step, 0)

    def corner_step(k, carry):
        zz = (z + k) % n_z
        relay(slot_of(1 - x, c, 1 - y, zz), sends_corner(k), x_is_query, x == 0, sends_corner_halves(k))
        relay(slot_of(x, 1 - c, 1 - y, zz), [], sib_is_query)
        relay(slot_of(1 - x, 1 - c, y, zz), [], diagonal_is_query)
        return carry

    lax.fori_loop(0, n_z, corner_step, 0)

    def last_step(k, carry):
        slot = slot_of(1 - x, 1 - c, 1 - y, (z + k) % n_z)
        relay(slot, [], diagonal_is_query, x == 0)
        return carry

    lax.fori_loop(0, n_z, last_step, 0)

    def own_step(h, carry):
        queries = proj[h].astype(jnp.float32)
        keys = proj[HEADS + h].astype(jnp.float32)
        strength = silu(jnp.sum(queries * keys, axis=-1, keepdims=True) * scale)
        own[h] = strength * proj[2 * HEADS + h].astype(jnp.float32)
        return carry

    lax.fori_loop(0, HEADS, own_step, 0)

    def return_step(k, carry):
        answer_copy(k).wait_recv()
        return carry

    lax.fori_loop(1, n_usr, return_step, 0)

    def tile_step(t, carry):
        holder = user_ref[0, t]
        combined = jnp.concatenate(
            [returned[holder, h].astype(jnp.float32) + own[h, t] for h in range(HEADS)], axis=-1
        )
        units = jnp.concatenate([proj[3 * HEADS + h, t] for h in range(HEADS)], axis=-1)
        gated[t] = (norm_rows(combined) * units.astype(jnp.float32)).astype(jnp.bfloat16)
        return carry

    lax.fori_loop(0, tiles, tile_step, 0)

    slots_here = lax.broadcasted_iota(jnp.int32, (tile_rows, 1), 0)
    for lo in range(0, model_width, 256):
        weights = wo_all[:, :, lo : lo + 256].reshape(model_width, 256)
        mixed = jnp.dot(
            gated[...].reshape(row_total, model_width), weights, preferred_element_type=jnp.float32
        )
        for t in range(tiles):
            rows = slice(t * tile_rows, (t + 1) * tile_rows)
            total = mixed[rows] + cand_ref[rows, lo : lo + 256].astype(jnp.float32)
            out_ref[rows, lo : lo + 256] = jnp.where(slots_here < count_ref[t], total, 0.0).astype(
                jnp.bfloat16
            )

    each(o_copy, sends_own() + sends_across(), sent)

    @pl.when(jnp.logical_not(is_query))
    def _():
        each(w_copy, sends_own() + sends_across(), sent)

    def sent_line(zz, carry):
        @pl.when(zz != z)
        def _():
            each(o_copy, sends_line(zz), sent)

        @pl.when((zz != z) & jnp.logical_not(is_query))
        def _():
            each(w_copy, sends_line(zz), sent)

        @pl.when(c == 0)
        def _():
            for part in range(2):
                each(w_copy, sends_query(zz, part) + sends_query_y(zz, part), sent)

        return carry

    def sent_rest(k, carry):
        by_y, by_x = sends_y_halves(k), sends_x_halves(k) + sends_corner_halves(k)
        each(o_copy, sends_y(k) + sends_x(k) + sends_corner(k), sent)

        @pl.when(jnp.logical_not(is_query))
        def _():
            each(w_copy, by_y, sent)

        @pl.when(jnp.logical_not(x_is_query))
        def _():
            each(w_copy, by_x, sent)

        return carry

    def sent_exchange(k, carry):
        query_copy(k).wait_send()
        answer_copy(k).wait_send()
        return carry

    lax.fori_loop(0, n_z, sent_line, 0)
    lax.fori_loop(0, n_z, sent_rest, 0)
    lax.fori_loop(1, n_usr, sent_exchange, 0)


def fused_shards(
    candidates, hist_kv, hist_len, block_mask, tile_user, tile_count, weight_in, weight_out
):
    row_total, model_width = candidates.shape
    n_usr, n_grp = lax.axis_size("usr"), lax.axis_size("grp")
    devices = n_usr * n_grp
    depth, width = weight_in.shape
    out_rows = weight_out.shape[0]
    tiles = tile_user.shape[0]
    tile_rows = row_total // tiles
    sends = 5 + 23 * (n_usr // 2)
    exchange = pltpu.VMEM((n_usr, HEADS, tile_rows, width), jnp.bfloat16)
    dma = pltpu.SemaphoreType.DMA
    in_any = pl.BlockSpec(memory_space=pl.ANY)
    in_vmem = pl.BlockSpec(memory_space=pltpu.VMEM)
    in_smem = pl.BlockSpec(memory_space=pltpu.SMEM)
    flops = 2 * row_total * model_width * model_width * 5 + 8 * n_usr * tile_rows * hist_kv.shape[1] * model_width
    return pl.pallas_call(
        functools.partial(layer_kernel, n_usr),
        out_shape=jax.ShapeDtypeStruct((row_total, model_width), jnp.bfloat16),
        in_specs=[in_any, in_any, in_smem, in_smem, in_smem, in_smem, in_any, in_any],
        out_specs=in_vmem,
        scratch_shapes=[
            pltpu.VMEM((row_total, model_width), jnp.bfloat16),
            pltpu.VMEM(hist_kv.shape, jnp.bfloat16),
            pltpu.VMEM((HEADS, width, hist_kv.shape[1]), jnp.bfloat16),
            pltpu.VMEM((row_total, model_width), jnp.bfloat16),
            pltpu.VMEM((devices, depth, width), jnp.bfloat16),
            pltpu.VMEM((devices, out_rows, model_width), jnp.bfloat16),
            pltpu.VMEM((devices, tiles, tile_rows, width), jnp.bfloat16),
            pltpu.VMEM((HEADS, tiles, tile_rows, width), jnp.float32),
            exchange,
            exchange,
            exchange,
            exchange,
            pltpu.VMEM((tiles, tile_rows, model_width), jnp.bfloat16),
            dma((devices, 2)),
            dma((devices,)),
            dma((sends,)),
            dma((5 + 9 * (n_usr // 2),)),
            dma((n_usr,)),
            dma((n_usr,)),
            dma((n_usr,)),
            dma((n_usr,)),
            dma((4,)),
        ],
        compiler_params=pltpu.CompilerParams(
            collective_id=0, has_side_effects=True, vmem_limit_bytes=60 * 1024 * 1024
        ),
        cost_estimate=pl.CostEstimate(flops=flops, bytes_accessed=4 * 1024 * 1024, transcendentals=0),
    )(candidates, hist_kv, hist_len, block_mask, tile_user.T, tile_count, weight_in, weight_out)


def solution(mesh):
    in_specs = (
        P(("grp", "usr"), None),
        P(("grp", "usr"), None, None),
        P(("grp", "usr")),
        P(("grp", "usr"), None),
        P(("grp", "usr"), None),
        P(("grp", "usr")),
        P(None, ("grp", "usr")),
        P(("grp", "usr"), None),
    )
    out_specs = P(("grp", "usr"), None)
    fits = mesh.shape["grp"] == 4 and mesh.shape["usr"] == HEADS
    body = fused_shards if fits else shards
    return jax.shard_map(body, mesh=mesh, in_specs=in_specs, out_specs=out_specs, check_vma=False)
```

```python
import functools
import math

import jax
import jax.numpy as jnp
from jax import lax
from jax.experimental import pallas as pl
from jax.experimental.pallas import tpu as pltpu
from jax.sharding import PartitionSpec as P

HEADS = 8
BLK = 128
MESH = pl.DeviceIdType.MESH


def norm_rows(values_in):
    centred = values_in - jnp.mean(values_in, axis=-1, keepdims=True)
    variance = jnp.mean(centred * centred, axis=-1, keepdims=True)
    return centred * lax.rsqrt(variance + 1e-05)


def attend_rows(query_rows, hist_keys, hist_values, live_items, score_scale):
    row_total = query_rows.shape[0]
    model_width = query_rows.shape[1]
    head_dim = model_width // HEADS
    query_heads = query_rows.reshape(row_total, HEADS, head_dim)
    key_heads = hist_keys.reshape(-1, HEADS, head_dim)
    value_heads = hist_values.reshape(-1, HEADS, head_dim)
    scores = (
        jnp.einsum("nhd,lhd->hnl", query_heads, key_heads, preferred_element_type=jnp.float32)
        * score_scale
    )
    weights = (jax.nn.silu(scores) * live_items).astype(jnp.bfloat16)
    attended = jnp.einsum("hnl,lhd->nhd", weights, value_heads, preferred_element_type=jnp.float32)
    return attended.reshape(row_total, model_width)


def own_term(queries, self_keys, self_values, score_scale):
    row_total = queries.shape[0]
    products = (queries.astype(jnp.float32) * self_keys.astype(jnp.float32)).reshape(
        row_total, HEADS, -1
    )
    strength = jax.nn.silu(jnp.sum(products, axis=2) * score_scale)
    value_heads = self_values.astype(jnp.float32).reshape(row_total, HEADS, -1)
    return (strength[:, :, None] * value_heads).reshape(row_total, -1)


def holder_attend(incoming, hist_keys, hist_values, live_items, score_scale):
    slot_total, item_count, model_width = incoming.shape
    per_group = math.gcd(slot_total, max(1, 512 // item_count))
    group_total = slot_total // per_group

    def answer_rows(row_block):
        return attend_rows(row_block, hist_keys, hist_values, live_items, score_scale).astype(
            jnp.bfloat16
        )

    row_blocks = incoming.reshape(group_total, per_group * item_count, model_width)
    answered = lax.map(answer_rows, row_blocks)
    return answered.reshape(slot_total, item_count, model_width)


def shards(candidates, hist_kv, hist_len, block_mask, tile_user, tile_count, weight_in, weight_out):
    row_total, model_width = candidates.shape
    tiles_here = tile_user.shape[0]
    tile_rows = row_total // tiles_here
    score_scale = (model_width // HEADS) ** (-0.5)
    holders = lax.axis_size("usr")
    normed = norm_rows(candidates.astype(jnp.float32)).astype(jnp.bfloat16)
    projected = jax.nn.silu(
        jnp.dot(
            normed,
            lax.all_gather(weight_in, ("grp", "usr"), axis=1, tiled=True),
            preferred_element_type=jnp.float32,
        )
    ).astype(jnp.bfloat16)
    queries = projected[:, :model_width]
    self_keys = projected[:, model_width : 2 * model_width]
    self_values = projected[:, 2 * model_width : 3 * model_width]
    gate_units = projected[:, 3 * model_width :]
    own_part = own_term(queries, self_keys, self_values, score_scale)
    tile_dest = tile_user[:, 0]
    outgoing = jnp.zeros((holders, tile_rows, model_width), jnp.bfloat16)
    outgoing = outgoing.at[tile_dest].set(queries.reshape(tiles_here, tile_rows, model_width))
    hist_keys = hist_kv[0, :, :model_width]
    hist_values = hist_kv[0, :, model_width:]
    positions = jnp.arange(hist_kv.shape[1], dtype=jnp.int32)
    live_items = ((positions < hist_len[0]) & (jnp.repeat(block_mask[0], BLK) > 0)).astype(
        jnp.float32
    )
    incoming = lax.all_to_all(outgoing, "usr", split_axis=0, concat_axis=0, tiled=True)
    returned = lax.all_to_all(
        holder_attend(incoming, hist_keys, hist_values, live_items, score_scale),
        "usr",
        split_axis=0,
        concat_axis=0,
        tiled=True,
    )
    history = returned[tile_dest].reshape(row_total, model_width)
    combined = history.astype(jnp.float32) + own_part
    gated_rows = (norm_rows(combined) * gate_units.astype(jnp.float32)).astype(jnp.bfloat16)
    mixed_rows = jnp.dot(
        gated_rows,
        lax.all_gather(weight_out, ("grp", "usr"), axis=0, tiled=True),
        preferred_element_type=jnp.float32,
    )
    mixed_rows = mixed_rows + candidates.astype(jnp.float32)
    live_rows = (jnp.arange(tile_rows, dtype=jnp.int32)[None, :] < tile_count[:, None]).reshape(-1)
    return jnp.where(live_rows[:, None], mixed_rows, 0.0).astype(jnp.bfloat16)


def silu(v):
    half = 0.5 * v
    return half + half * jnp.tanh(half)


def layer_kernel(
    n_usr,
    cand_hbm,
    kv_hbm,
    len_ref,
    mask_ref,
    user_ref,
    count_ref,
    win_hbm,
    wout_hbm,
    out_ref,
    cand_ref,
    kv_ref,
    key_heads,
    normed,
    w_all,
    wo_all,
    proj,
    own,
    outgoing,
    incoming,
    answers,
    returned,
    gated,
    w_recv,
    o_recv,
    w_send,
    o_send,
    q_recv,
    q_send,
    a_recv,
    a_send,
    load_sem,
):
    depth, width = win_hbm.shape
    out_rows = wout_hbm.shape[0]
    row_total, model_width = cand_ref.shape
    tiles = user_ref.shape[1]
    tile_rows = row_total // tiles
    items = kv_ref.shape[1]
    scale = width ** (-0.5)
    g, u = lax.axis_index("grp"), lax.axis_index("usr")
    n_z = n_usr // 2
    x, c = g // 2, g % 2
    z, y = u // 2, u % 2
    to_x = ((1 - x) * 2 + c, u)
    to_c = (x * 2 + (1 - c), u)
    to_y = (g, z * 2 + (1 - y))

    def slot_of(xx, cc, yy, zz):
        return (xx * 2 + cc) * n_usr + zz * 2 + yy

    def w_copy(slot, part, target, sem):
        half = depth // 2
        lo, size = (0, depth) if part is None else (part * half, half)
        view = w_all.at[slot, pl.ds(lo, size), :]
        return pltpu.make_async_remote_copy(
            src_ref=view,
            dst_ref=view,
            send_sem=w_send.at[sem],
            recv_sem=w_recv.at[slot, part or 0],
            device_id=target,
            device_id_type=MESH,
        )

    def o_copy(slot, part, target, sem):
        view = wo_all.at[slot]
        return pltpu.make_async_remote_copy(
            src_ref=view,
            dst_ref=view,
            send_sem=o_send.at[sem],
            recv_sem=o_recv.at[slot],
            device_id=target,
            device_id_type=MESH,
        )

    is_query, x_is_query = (x == 0) & (c == 0), (x == 1) & (c == 0)
    sib_is_query, diagonal_is_query = (x == 0) & (c == 1), (x == 1) & (c == 1)

    def along_z(slot, zz, base):
        up, down = (zz <= z) & (z + 1 < n_z), (zz >= z) & (z > 0)
        return [
            (up, slot, None, (g, (z + 1) * 2 + y), base),
            (down, slot, None, (g, (z - 1) * 2 + y), base + 1),
        ]

    def sends_own():
        me = slot_of(x, c, y, z)
        return along_z(me, z, 0) + [(None, me, None, to_y, 2), (None, me, None, to_c, 3)]

    def sends_across():
        return [(None, slot_of(x, c, y, z), None, to_x, 4)]

    def sends_line(zz):
        slot = slot_of(x, c, y, zz)
        base = 5 + zz * 5
        return along_z(slot, zz, base) + [
            (None, slot, None, to_x, base + 2),
            (None, slot, None, to_y, base + 3),
            (None, slot, None, to_c, base + 4),
        ]

    def sends_y(k):
        slot = slot_of(x, c, 1 - y, (z + k) % n_z)
        base = 5 + n_z * 5 + k * 2
        return [(None, slot, None, to_x, base), (None, slot, None, to_c, base + 1)]

    def sends_x(k):
        slot = slot_of(1 - x, c, y, (z + k) % n_z)
        return [(None, slot, None, to_c, 5 + n_z * 7 + k)]

    def sends_corner(k):
        slot = slot_of(1 - x, c, 1 - y, (z + k) % n_z)
        return [(None, slot, None, to_c, 5 + n_z * 8 + k)]

    def sends_y_halves(k):
        whole, relayed = sends_y(k)
        return [(x == 0,) + whole[1:], (x == 1, whole[1], 0) + whole[3:], relayed]

    def sends_x_halves(k):
        slot = slot_of(1 - x, c, y, (z + k) % n_z)
        return sends_x(k) + [(x == 0, slot, 1, to_y, 5 + n_z * 21 + k)]

    def sends_corner_halves(k):
        slot, base = slot_of(1 - x, c, 1 - y, (z + k) % n_z), 5 + n_z * 8 + k
        return [
            (x == 1, slot, None, to_c, base),
            (x == 0, slot, 0, to_c, base),
            (x == 0, slot, 1, to_c, 5 + n_z * 22 + k),
        ]

    def sends_query(zz, part):
        slot = slot_of(0, 0, y, zz)
        base = 5 + n_z * 9 + zz * 10 + part * 5
        up, down = (x == 0) & (zz <= z) & (z + 1 < n_z), (x == 0) & (zz >= z) & (z > 0)
        return [
            (up, slot, part, (g, (z + 1) * 2 + y), base),
            (down, slot, part, (g, (z - 1) * 2 + y), base + 1),
            (x == 0, slot, part, to_x, base + 2),
            (None, slot, part, to_y, base + 3),
            (None, slot, part, to_c, base + 4),
        ]

    def sends_query_y(k, part):
        slot = slot_of(0, 0, 1 - y, (z + k) % n_z)
        return [(None, slot, part, to_c, 5 + n_z * 19 + k * 2 + part)]

    early, late = x == 1, (x == 0) & (c == 1)

    def not_y(listed):
        return [entry for entry in listed if entry[3] is not to_y]

    def only_y(listed):
        return [entry for entry in listed if entry[3] is to_y]

    def each(copy, listed, act):
        for needed, slot, part, target, sem in listed:
            if needed is None:
                act(copy(slot, part, target, sem))
            else:
                pl.when(needed)(lambda a=(slot, part, target, sem): act(copy(*a)))

    def start(descriptor):
        descriptor.start()

    def sent(descriptor):
        descriptor.wait_send()

    def arrived(copy, slot, part):
        copy(slot, part, to_c, 0).wait_recv()

    def project(slot):
        block = silu(jnp.dot(normed[...], w_all[slot], preferred_element_type=jnp.float32))
        proj[slot] = block.astype(jnp.bfloat16).reshape(tiles, tile_rows, width)

    def relay(slot, listed, skip, halves=None, w_listed=None):
        w_listed = listed if w_listed is None else w_listed
        if halves is None:

            @pl.when(jnp.logical_not(skip))
            def _():
                arrived(w_copy, slot, None)
                each(w_copy, w_listed, start)
        else:

            @pl.when(jnp.logical_not(skip) & halves)
            def _():
                for part in range(2):
                    arrived(w_copy, slot, part)
                    each(w_copy, [entry for entry in w_listed if entry[2] == part], start)

            @pl.when(jnp.logical_not(skip | halves))
            def _():
                arrived(w_copy, slot, None)
                each(w_copy, [entry for entry in w_listed if entry[2] is None], start)

        arrived(o_copy, slot, None)
        each(o_copy, listed, start)

        @pl.when(jnp.logical_not(skip))
        def _():
            project(slot)

    barrier = pltpu.get_barrier_semaphore()
    peers = [to_x, to_c] + [(g, (u + k) % n_usr) for k in range(1, n_usr)]
    for peer in peers:
        pl.semaphore_signal(barrier, inc=1, device_id=peer, device_id_type=MESH)
    mine = slot_of(x, c, y, z)
    loads = [
        pltpu.make_async_copy(cand_hbm, cand_ref, load_sem.at[0]),
        pltpu.make_async_copy(win_hbm, w_all.at[mine], load_sem.at[1]),
        pltpu.make_async_copy(wout_hbm, wo_all.at[mine], load_sem.at[2]),
        pltpu.make_async_copy(kv_hbm, kv_ref, load_sem.at[3]),
    ]
    for load in loads:
        load.start()
    loads[0].wait()
    normed[...] = norm_rows(cand_ref[...].astype(jnp.float32)).astype(jnp.bfloat16)
    loads[1].wait()
    pl.semaphore_wait(barrier, len(peers))

    @pl.when(early)
    def _():
        each(w_copy, sends_across() + not_y(sends_own()), start)

    def query_relay(zz, known):
        slot = slot_of(0, 0, y, zz)

        for part in range(2):

            @pl.when(jnp.logical_not(known))
            def _(part=part):
                arrived(w_copy, slot, part)

            @pl.when(c == 0)
            def _(part=part):
                each(w_copy, sends_query(zz, part), start)

    query_relay(z, is_query)
    project(slot_of(0, 0, y, z))

    def query_line(k, carry):
        for zz in (z - k, z + k):

            @pl.when((zz >= 0) & (zz < n_z))
            def _(zz=zz):
                query_relay(zz, False)
                project(slot_of(0, 0, y, zz))

            @pl.when((zz >= 0) & (zz < n_z) & early)
            def _(zz=zz):
                slot = slot_of(x, c, y, zz)
                arrived(w_copy, slot, None)
                each(w_copy, not_y(sends_line(zz)), start)
                project(slot)

        return carry

    lax.fori_loop(1, n_z, query_line, 0)

    def query_side(k, carry):
        slot = slot_of(0, 0, 1 - y, (z + k) % n_z)
        for part in range(2):
            arrived(w_copy, slot, part)

            @pl.when(c == 0)
            def _(part=part):
                each(w_copy, sends_query_y(k, part), start)

        project(slot)
        return carry

    lax.fori_loop(0, n_z, query_side, 0)

    def query_copy(k):
        holder = ((z + k // 2) % n_z) * 2 + (y + k) % 2
        return pltpu.make_async_remote_copy(
            src_ref=outgoing.at[holder],
            dst_ref=incoming.at[u],
            send_sem=q_send.at[k],
            recv_sem=q_recv.at[k],
            device_id=(g, holder),
            device_id_type=MESH,
        )

    def source_of(k):
        return ((z + n_z - k // 2) % n_z) * 2 + (y + k) % 2

    def answer_copy(k):
        source = source_of(k)
        return pltpu.make_async_remote_copy(
            src_ref=answers.at[source],
            dst_ref=returned.at[u],
            send_sem=a_send.at[k],
            recv_sem=a_recv.at[k],
            device_id=(g, source),
            device_id_type=MESH,
        )

    def tile_for(holder):
        chosen = 0
        for t in range(tiles):
            chosen = jnp.where(user_ref[0, t] == holder, t, chosen)
        return chosen

    def dispatch_step(k, carry):
        holder = ((z + k // 2) % n_z) * 2 + (y + k) % 2
        tile = tile_for(holder)
        for h in range(HEADS):
            outgoing[holder, h] = proj[h, tile]
        query_copy(k).start()
        return carry

    lax.fori_loop(1, n_usr, dispatch_step, 0)
    own_tile = tile_for(u)
    for h in range(HEADS):
        incoming[u, h] = proj[h, own_tile]

    positions = lax.broadcasted_iota(jnp.int32, (1, items), 1)
    kept = jnp.zeros((1, items), jnp.int32)
    for b in range(items // BLK):
        kept = jnp.where(positions // BLK == b, mask_ref[0, b], kept)
    live = jnp.where((positions < len_ref[0]) & (kept > 0), 1.0, 0.0)

    loads[3].wait()
    for h in range(HEADS):
        key_heads[h] = kv_ref[0, :, h * width : (h + 1) * width].T

    def attend(slot, dest):
        for h in range(HEADS):
            values = kv_ref[0, :, model_width + h * width : model_width + (h + 1) * width]
            scores = jnp.dot(incoming[slot, h], key_heads[h], preferred_element_type=jnp.float32)
            weights = (silu(scores * scale) * live).astype(jnp.bfloat16)
            dest[slot, h] = jnp.dot(weights, values, preferred_element_type=jnp.float32).astype(
                jnp.bfloat16
            )

    def answer(k):
        query_copy(k).wait_recv()
        attend(source_of(k), answers)
        answer_copy(k).start()

    @pl.when(late)
    def _():
        each(w_copy, sends_own() + sends_across(), start)

    @pl.when(early)
    def _():
        each(w_copy, only_y(sends_own()), start)

    def line_y(zz, carry):
        @pl.when(early & (zz != z))
        def _():
            each(w_copy, only_y(sends_line(zz)), start)

        return carry

    lax.fori_loop(0, n_z, line_y, 0)

    @pl.when(jnp.logical_not(is_query))
    def _():
        project(mine)

    loads[2].wait()
    each(o_copy, sends_own() + sends_across(), start)

    attend(u, returned)

    def line_step(k, carry):
        answer(k)
        for zz in (z - k, z + k):

            @pl.when((zz >= 0) & (zz < n_z))
            def _(zz=zz):
                relay(slot_of(x, c, y, zz), sends_line(zz), jnp.logical_not(late))

        return carry

    lax.fori_loop(1, n_z, line_step, 0)

    def side_step(k, carry):
        zz = (z + k) % n_z
        relay(slot_of(x, c, 1 - y, zz), sends_y(k), is_query, None, sends_y_halves(k))
        relay(slot_of(1 - x, c, y, zz), sends_x(k), x_is_query, None, sends_x_halves(k))
        relay(slot_of(x, 1 - c, y, zz), [], sib_is_query)
        answer(n_z + k)
        return carry

    lax.fori_loop(0, n_z, side_step, 0)

    def corner_step(k, carry):
        zz = (z + k) % n_z
        relay(slot_of(1 - x, c, 1 - y, zz), sends_corner(k), x_is_query, x == 0, sends_corner_halves(k))
        relay(slot_of(x, 1 - c, 1 - y, zz), [], sib_is_query)
        relay(slot_of(1 - x, 1 - c, y, zz), [], diagonal_is_query)
        return carry

    lax.fori_loop(0, n_z, corner_step, 0)

    def last_step(k, carry):
        slot = slot_of(1 - x, 1 - c, 1 - y, (z + k) % n_z)
        relay(slot, [], diagonal_is_query, x == 0)
        return carry

    lax.fori_loop(0, n_z, last_step, 0)

    def own_step(h, carry):
        queries = proj[h].astype(jnp.float32)
        keys = proj[HEADS + h].astype(jnp.float32)
        strength = silu(jnp.sum(queries * keys, axis=-1, keepdims=True) * scale)
        own[h] = strength * proj[2 * HEADS + h].astype(jnp.float32)
        return carry

    lax.fori_loop(0, HEADS, own_step, 0)

    def return_step(k, carry):
        answer_copy(k).wait_recv()
        return carry

    lax.fori_loop(1, n_usr, return_step, 0)

    def tile_step(t, carry):
        holder = user_ref[0, t]
        combined = jnp.concatenate(
            [returned[holder, h].astype(jnp.float32) + own[h, t] for h in range(HEADS)], axis=-1
        )
        units = jnp.concatenate([proj[3 * HEADS + h, t] for h in range(HEADS)], axis=-1)
        gated[t] = (norm_rows(combined) * units.astype(jnp.float32)).astype(jnp.bfloat16)
        return carry

    lax.fori_loop(0, tiles, tile_step, 0)

    slots_here = lax.broadcasted_iota(jnp.int32, (tile_rows, 1), 0)
    for lo in range(0, model_width, 256):
        weights = wo_all[:, :, lo : lo + 256].reshape(model_width, 256)
        mixed = jnp.dot(
            gated[...].reshape(row_total, model_width), weights, preferred_element_type=jnp.float32
        )
        for t in range(tiles):
            rows = slice(t * tile_rows, (t + 1) * tile_rows)
            total = mixed[rows] + cand_ref[rows, lo : lo + 256].astype(jnp.float32)
            out_ref[rows, lo : lo + 256] = jnp.where(slots_here < count_ref[t], total, 0.0).astype(
                jnp.bfloat16
            )

    each(o_copy, sends_own() + sends_across(), sent)

    @pl.when(jnp.logical_not(is_query))
    def _():
        each(w_copy, sends_own() + sends_across(), sent)

    def sent_line(zz, carry):
        @pl.when(zz != z)
        def _():
            each(o_copy, sends_line(zz), sent)

        @pl.when((zz != z) & jnp.logical_not(is_query))
        def _():
            each(w_copy, sends_line(zz), sent)

        @pl.when(c == 0)
        def _():
            for part in range(2):
                each(w_copy, sends_query(zz, part) + sends_query_y(zz, part), sent)

        return carry

    def sent_rest(k, carry):
        by_y, by_x = sends_y_halves(k), sends_x_halves(k) + sends_corner_halves(k)
        each(o_copy, sends_y(k) + sends_x(k) + sends_corner(k), sent)

        @pl.when(jnp.logical_not(is_query))
        def _():
            each(w_copy, by_y, sent)

        @pl.when(jnp.logical_not(x_is_query))
        def _():
            each(w_copy, by_x, sent)

        return carry

    def sent_exchange(k, carry):
        query_copy(k).wait_send()
        answer_copy(k).wait_send()
        return carry

    lax.fori_loop(0, n_z, sent_line, 0)
    lax.fori_loop(0, n_z, sent_rest, 0)
    lax.fori_loop(1, n_usr, sent_exchange, 0)


def fused_shards(
    candidates, hist_kv, hist_len, block_mask, tile_user, tile_count, weight_in, weight_out
):
    row_total, model_width = candidates.shape
    n_usr, n_grp = lax.axis_size("usr"), lax.axis_size("grp")
    devices = n_usr * n_grp
    depth, width = weight_in.shape
    out_rows = weight_out.shape[0]
    tiles = tile_user.shape[0]
    tile_rows = row_total // tiles
    sends = 5 + 23 * (n_usr // 2)
    exchange = pltpu.VMEM((n_usr, HEADS, tile_rows, width), jnp.bfloat16)
    dma = pltpu.SemaphoreType.DMA
    in_any = pl.BlockSpec(memory_space=pl.ANY)
    in_vmem = pl.BlockSpec(memory_space=pltpu.VMEM)
    in_smem = pl.BlockSpec(memory_space=pltpu.SMEM)
    flops = 2 * row_total * model_width * model_width * 5 + 8 * n_usr * tile_rows * hist_kv.shape[1] * model_width
    return pl.pallas_call(
        functools.partial(layer_kernel, n_usr),
        out_shape=jax.ShapeDtypeStruct((row_total, model_width), jnp.bfloat16),
        in_specs=[in_any, in_any, in_smem, in_smem, in_smem, in_smem, in_any, in_any],
        out_specs=in_vmem,
        scratch_shapes=[
            pltpu.VMEM((row_total, model_width), jnp.bfloat16),
            pltpu.VMEM(hist_kv.shape, jnp.bfloat16),
            pltpu.VMEM((HEADS, width, hist_kv.shape[1]), jnp.bfloat16),
            pltpu.VMEM((row_total, model_width), jnp.bfloat16),
            pltpu.VMEM((devices, depth, width), jnp.bfloat16),
            pltpu.VMEM((devices, out_rows, model_width), jnp.bfloat16),
            pltpu.VMEM((devices, tiles, tile_rows, width), jnp.bfloat16),
            pltpu.VMEM((HEADS, tiles, tile_rows, width), jnp.float32),
            exchange,
            exchange,
            exchange,
            exchange,
            pltpu.VMEM((tiles, tile_rows, model_width), jnp.bfloat16),
            dma((devices, 2)),
            dma((devices,)),
            dma((sends,)),
            dma((5 + 9 * (n_usr // 2),)),
            dma((n_usr,)),
            dma((n_usr,)),
            dma((n_usr,)),
            dma((n_usr,)),
            dma((4,)),
        ],
        compiler_params=pltpu.CompilerParams(
            collective_id=0, has_side_effects=True, vmem_limit_bytes=60 * 1024 * 1024
        ),
        cost_estimate=pl.CostEstimate(flops=flops, bytes_accessed=4 * 1024 * 1024, transcendentals=0),
    )(candidates, hist_kv, hist_len, block_mask, tile_user.T, tile_count, weight_in, weight_out)


def solution(mesh):
    in_specs = (
        P(("grp", "usr"), None),
        P(("grp", "usr"), None, None),
        P(("grp", "usr")),
        P(("grp", "usr"), None),
        P(("grp", "usr"), None),
        P(("grp", "usr")),
        P(None, ("grp", "usr")),
        P(("grp", "usr"), None),
    )
    out_specs = P(("grp", "usr"), None)
    fits = mesh.shape["grp"] == 4 and mesh.shape["usr"] == HEADS
    body = fused_shards if fits else shards
    return jax.shard_map(body, mesh=mesh, in_specs=in_specs, out_specs=out_specs, check_vma=False)
```
